128 devices in a mesh: tx: 8 (over x, core), ty: 16 (over z, y).
Axes of the slice: x: 4, y: 4, z: 4, core: 2. Of those that a mesh axis runs over, the one named last changes fastest.
Arguments:
- features: bfloat16 [512, 64, 512], P(('tx', 'ty')), may hold values from -6 to 6
- weights: bfloat16 [3, 27, 64, 64], replicated, may hold values from -0.4375 to 0.4375
- cotangent: bfloat16 [512, 64, 512], P(('tx', 'ty')), may hold values from -6 to 6
- neighbours: int32 [512, 27], P(('tx', 'ty')), may hold values from -1 to 511, as said below
Outputs:
- out: bfloat16 [512, 64, 512], P(('tx', 'ty'))
- weight_grads: float32 [3, 27, 64, 64], replicated
The draws below stay inside these ranges and needn't reach their ends.
Inputs may be any that keep to these rules, and one draw needn't show every extreme that they name: `neighbours`: blocks lie on a grid of 16 x 2 * 16 x 2 block positions. The device at (r, c) of the tx x ty mesh holds slots from (r * 16 + c) * 4 on, placed at distinct positions whose first two coordinates lie in [2r, 2r+2) x [2c, 2c+2). A device's live slots come first. Devices (r, c) and (r, (c + 8) mod 16) are partners: in each pair one holds at most 2 live slots. Some device holds 4 live slots and its partner exactly 2.
All inputs are finite; a program needn't handle non-finite values.
Results may differ from the reference program's by a relative error of at most 0.013.
Values may be sent and summed in bfloat16 or wider, within the bound.
A program may use at most 128 MiB of HBM per device.

```python
import math
import jax
import jax.numpy as jnp

FEATURE_CHANNELS = 64
BLK = 8
SLOTS = 4
LAYERS = 3
LEND = 1
ROWS_T = 8
COLS_T = 16
GZ = 2
BLOCK_CELLS = 512
BLOCK_SLOT_COUNT = 512


def draw_neighbours(key, part):
    key = jax.random.fold_in(key, 7)
    key_one, key_two, key_three, key_four = jax.random.split(key, 4)
    half_cols = COLS_T // 2
    larger = jax.random.randint(key_one, (ROWS_T, half_cols), 1, SLOTS + 1)
    smaller = jax.random.randint(key_two, (ROWS_T, half_cols), 1, SLOTS - 2 * LEND + 1)
    larger = larger.at[0, 0].set(SLOTS)
    smaller = smaller.at[0, 0].set(SLOTS - 2 * LEND)
    axes_exchanged = jax.random.randint(key_three, (ROWS_T, half_cols), 0, 2)
    lower_half = jnp.where(axes_exchanged == 1, larger, smaller)
    upper_half = jnp.where(axes_exchanged == 1, smaller, larger)
    counts = jnp.concatenate([lower_half, upper_half], axis=1).reshape(-1)
    tile_total = ROWS_T * COLS_T
    places = 4 * GZ
    orders = jax.vmap(lambda inner_key: jax.random.permutation(inner_key, places))(jax.random.split(key_four, tile_total))
    chosen = orders[:, :SLOTS]
    tile_id = jnp.arange(tile_total, dtype=jnp.int32)[:, None]
    slot_id = jnp.arange(SLOTS, dtype=jnp.int32)[None, :]
    is_live = slot_id < counts[:, None]
    cell_x = tile_id // COLS_T * 2 + chosen // (2 * GZ)
    cell_y = tile_id % COLS_T * 2 + chosen // GZ % 2
    cell_z = chosen % GZ
    slot_ident = (tile_id * SLOTS + slot_id).astype(jnp.int32)
    extent_x = 2 * ROWS_T
    span_along_y = 2 * COLS_T
    cell_total = extent_x * span_along_y * GZ
    flattened_cell = jnp.where(is_live, (cell_x * span_along_y + cell_y) * GZ + cell_z, cell_total)
    occupant = jnp.full((cell_total,), -1, jnp.int32).at[flattened_cell.reshape(-1)].set(slot_ident.reshape(-1), mode='drop')
    columns = []
    for step_x in (-1, 0, 1):
        for step_y in (-1, 0, 1):
            for step_z in (-1, 0, 1):
                near_x = cell_x + step_x
                near_y = cell_y + step_y
                near_z = cell_z + step_z
                inside = (near_x >= 0) & (near_x < extent_x) & (near_y >= 0) & (near_y < span_along_y) & (near_z >= 0) & (near_z < GZ) & is_live
                cell_id = jnp.clip((near_x * span_along_y + near_y) * GZ + near_z, 0, cell_total - 1)
                columns.append(jnp.where(inside, occupant[cell_id], -1))
    return jnp.stack(columns, axis=-1).reshape(tile_total * SLOTS, 27).astype(jnp.int32)


def level_of(stream_key, dims, cuts, least, largest):
    gain = 1.0
    for axis_at, blocks in cuts:
        draws = jax.random.uniform(jax.random.fold_in(jax.random.fold_in(stream_key, 6), axis_at), (blocks,), jnp.float32, least / len(cuts), largest / len(cuts))
        gain = gain * jnp.repeat(jnp.exp(draws), dims[axis_at] // blocks).reshape((-1,) + (1,) * (len(dims) - 1 - axis_at))
    return gain


def bell_draw(rng, shape, deviation, reach, cuts=(), held_as=jnp.bfloat16):
    values = deviation * jax.random.normal(rng, shape, jnp.float32)
    if cuts:
        values = values * level_of(rng, shape, cuts, -0.22, 0.18)
    return jnp.clip(values, -reach, reach).astype(held_as)


def setup_inputs(seed: int = 0) -> dict:
    keys = jax.random.split(jax.random.key(seed), 5)
    features = bell_draw(keys[0], (BLOCK_SLOT_COUNT, FEATURE_CHANNELS, BLOCK_CELLS), 1.0, 6.0, ((0, 128),))
    weights = bell_draw(keys[1], (LAYERS, 27, FEATURE_CHANNELS, FEATURE_CHANNELS), (27 * FEATURE_CHANNELS // 8) ** -0.5, 0.4375)
    cotangent = bell_draw(keys[2], (BLOCK_SLOT_COUNT, FEATURE_CHANNELS, BLOCK_CELLS), 1.0, 6.0, ((0, 128),))
    neighbours = draw_neighbours(jax.random.fold_in(keys[4], 71), 0)
    return {"features": features, "weights": weights, "cotangent": cotangent, "neighbours": neighbours}


def offsets():
    return [(step_x, step_y, step_z) for step_x in (-1, 0, 1) for step_y in (-1, 0, 1) for step_z in (-1, 0, 1)]

def source_range(step):
    if step < 0:
        return slice(BLK - 1, BLK)
    if step > 0:
        return slice(0, 1)
    return slice(0, BLK)

def target_range(step):
    if step < 0:
        return slice(0, 1)
    if step > 0:
        return slice(BLK + 1, BLK + 2)
    return slice(1, BLK + 1)

def assemble(flat_field, neighbours):
    slot_total, channels = (flat_field.shape[0], flat_field.shape[1])
    volume = flat_field.reshape(slot_total, channels, BLK, BLK, BLK)
    padded = jnp.zeros((slot_total, channels, BLK + 2, BLK + 2, BLK + 2), jnp.bfloat16)
    for offset_id, (step_x, step_y, step_z) in enumerate(offsets()):
        region = volume[:, :, source_range(step_x), source_range(step_y), source_range(step_z)]
        neighbour_ids = neighbours[:, offset_id]
        portion = jnp.take(region, jnp.maximum(neighbour_ids, 0).astype(jnp.int32), axis=0)
        present = (neighbour_ids >= 0)[:, None, None, None, None]
        portion = jnp.where(present, portion, jnp.zeros_like(portion))
        padded = padded.at[:, :, target_range(step_x), target_range(step_y), target_range(step_z)].set(portion)
    return padded

def window_at(padded, step_x, step_y, step_z):
    slot_total, channels = (padded.shape[0], padded.shape[1])
    return padded[:, :, 1 + step_x:1 + step_x + BLK, 1 + step_y:1 + step_y + BLK, 1 + step_z:1 + step_z + BLK].reshape(slot_total, channels, BLK ** 3)

def convolve(padded, kernel):
    summed = jnp.zeros((padded.shape[0], kernel.shape[1], BLK ** 3), jnp.float32)
    for offset_id, (step_x, step_y, step_z) in enumerate(offsets()):
        window = window_at(padded, step_x, step_y, step_z).astype(jnp.float32)
        summed = summed + jnp.einsum('ki,biv->bkv', kernel[offset_id].astype(jnp.float32), window)
    return summed

def correlate(padded, delta_z):
    partials = []
    delta_wide = delta_z.astype(jnp.float32)
    for offset_id, (step_x, step_y, step_z) in enumerate(offsets()):
        window = window_at(padded, step_x, step_y, step_z).astype(jnp.float32)
        partials.append(jnp.einsum('bkv,biv->ki', delta_wide, window))
    return jnp.stack(partials)

def silu_slope(value):
    sigma = jax.nn.sigmoid(value)
    return sigma * (1.0 + value * (1.0 - sigma))

def reference(features, weights, cotangent, neighbours):
    inputs = []
    preacts = []
    activation = features
    for layer_id in range(LAYERS):
        padded = assemble(activation, neighbours)
        preact = convolve(padded, weights[layer_id])
        inputs.append(padded)
        preacts.append(preact)
        activation = jax.nn.silu(preact).astype(jnp.bfloat16)
    gradient = cotangent
    partials = [None] * LAYERS
    for layer_id in reversed(range(LAYERS)):
        delta_z = (gradient.astype(jnp.float32) * silu_slope(preacts[layer_id])).astype(jnp.bfloat16)
        partials[layer_id] = correlate(inputs[layer_id], delta_z)
        if layer_id > 0:
            flipped = jnp.transpose(weights[layer_id][::-1], (0, 2, 1))
            gradient = convolve(assemble(delta_z, neighbours), flipped).astype(jnp.bfloat16)
    scale_factor = 1.0 / math.sqrt(BLOCK_SLOT_COUNT * BLOCK_CELLS)
    return (activation, jnp.stack(partials) * scale_factor)
```

```python
import functools
import math

import jax
import jax.numpy as jnp
from jax import lax
from jax.experimental import pallas as pl
from jax.experimental.pallas import tpu as pltpu
from jax.sharding import PartitionSpec as P

BLK = 8
LAYERS = 3
F32 = jnp.float32
BF16 = jnp.bfloat16
MESH = pl.DeviceIdType.MESH
DIRS = [(-1, 0), (1, 0), (0, -1), (0, 1), (-1, -1), (-1, 1), (1, -1), (1, 1)]


def side(step):
    return 0 if step < 0 else 1


def lane_iota(shape):
    return lax.broadcasted_iota(jnp.int32, shape, len(shape) - 1)


def swap_halves(value):
    return pltpu.roll(value, 64, len(value.shape) - 1)


def pack_cols(face):
    low, high = face[0:4], face[4:8]
    packed = jnp.where(lane_iota(low.shape) < 64, low, swap_halves(high))
    return packed.reshape(32, 128).astype(BF16)


def unpack_cols(packed):
    wide = packed.astype(F32).reshape(4, 8, 128)
    return jnp.concatenate([wide, swap_halves(wide)], axis=0)


def triple(below, here, above):
    z = lax.broadcasted_iota(jnp.int32, here.shape, 1)
    lane = lane_iota(here.shape)
    down = pltpu.roll(jnp.where(z == 7, below, here), 1, 1)
    up = pltpu.roll(jnp.where(z == 0, above, here), 7, 1)
    first = jnp.where(lane < 64, down, swap_halves(here))
    second = jnp.where(lane < 64, up, 0.0)
    return jnp.concatenate([first, second], axis=2)


def sigmoid(value):
    return 1.0 / (1.0 + jnp.exp(-value))


def kernel(
    rows, cols, feat, w, cot, nbr, out, raw,
    idx, field, zp, pre, wf, wb, d3t, send_sem, recv_sem, *pools,
):
    px, py, pd, sd = pools[0:5], pools[5:10], pools[10:15], pools[15:20]
    r, c = lax.axis_index("tx"), lax.axis_index("ty")

    def peer(dr, dc):
        return (lax.rem(r + dr + rows, rows), lax.rem(c + dc + cols, cols))

    barrier = pltpu.get_barrier_semaphore()
    for dr, dc in DIRS:
        pl.semaphore_signal(barrier, inc=1, device_id=peer(dr, dc), device_id_type=MESH)

    def fill_idx(b, carry):
        for o in range(27):
            ox, oy = o // 9 - 1, o // 3 % 3 - 1
            n = nbr[b, o]
            there = n >= 0
            n = jnp.maximum(n, 0)
            slot = n & 3
            dev = n >> 2
            same_r, same_c = (dev // cols) == r, (dev % cols) == c
            base = (b * 27 + o) * 3
            if ox == 0 and oy == 0:
                idx[base] = jnp.where(there, slot, 4)
            elif oy == 0:
                idx[base] = jnp.where(there, slot + jnp.where(same_r, 0, 4), 8)
            elif ox == 0:
                idx[base] = jnp.where(there, slot + jnp.where(same_c, 0, 4), 8)
            else:
                idx[base] = jnp.where(there & same_c, slot + jnp.where(same_r, 0, 4), 8)
                idx[base + 1] = jnp.where(
                    there & same_r & jnp.logical_not(same_c), slot + 4, 8
                )
                idx[base + 2] = jnp.where(
                    there & jnp.logical_not(same_r) & jnp.logical_not(same_c), slot, 4
                )
        return carry

    lax.fori_loop(0, 4, fill_idx, 0)

    field[4] = jnp.zeros((64, 8, 128), F32)
    for e in range(5):
        for s in range(2):
            px[e][s, 8] = jnp.zeros((32, 128), BF16)
            py[e][s, 8] = jnp.zeros((32, 128), BF16)
        for q in range(4):
            pd[e][q, 4] = jnp.zeros((8, 128), F32)

    def load_field(source):
        def one(s, carry):
            wide = source[s].astype(F32)
            wide = jnp.concatenate([wide, jnp.zeros((64, 512), F32)], axis=0)
            field[s] = wide.T.reshape(64, 8, 128)
            return carry

        lax.fori_loop(0, 4, one, 0)

    def build_wf(layer):
        for dx in range(3):
            rows_here = []
            for dy in range(3):
                for dz in range(3):
                    rows_here.append(w[layer, 9 * dx + 3 * dy + dz])
                rows_here.append(jnp.zeros((64, 64), BF16))
            wf[dx * 64:(dx + 1) * 64, :] = jnp.concatenate(rows_here, axis=1)
        wf[192:256, :] = jnp.zeros((64, 768), BF16)

    def build_wb(layer):
        for dy in range(3):
            for dz in range(3):
                row = dy * 256 + dz * 64
                parts = [w[layer, 26 - (9 * dx + 3 * dy + dz)] for dx in range(3)]
                parts.append(jnp.zeros((64, 64), BF16))
                wb[row:row + 64, :] = jnp.concatenate(parts, axis=1)
            wb[dy * 256 + 192:dy * 256 + 256, :] = jnp.zeros((64, 256), BF16)

    def copies(e):
        made = []
        for k, (dr, dc) in enumerate(DIRS):
            if dc == 0:
                s = 0 if dr > 0 else 1
                src, dst = px[e].at[s, pl.ds(0, 4)], px[e].at[s, pl.ds(4, 4)]
            elif dr == 0:
                s = 0 if dc > 0 else 1
                src, dst = py[e].at[s, pl.ds(0, 4)], py[e].at[s, pl.ds(4, 4)]
            else:
                q = (0 if dr > 0 else 1) * 2 + (0 if dc > 0 else 1)
                src, dst = sd[e].at[q], pd[e].at[q, pl.ds(0, 4)]
            made.append(
                pltpu.make_async_remote_copy(
                    src_ref=src, dst_ref=dst, send_sem=send_sem.at[e, k],
                    recv_sem=recv_sem.at[e, k], device_id=peer(dr, dc), device_id_type=MESH,
                )
            )
        return made

    def faces_out(e):
        def one(s, carry):
            for sx in range(2):
                x = 7 if sx == 0 else 0
                face = field[s, pl.ds(x * 8, 8)]
                px[e][sx, s] = pack_cols(face)
                for sy in range(2):
                    y = 7 if sy == 0 else 0
                    sd[e][sx * 2 + sy, s] = face[y]
            for sy in range(2):
                y = 7 if sy == 0 else 0
                face = jnp.concatenate([field[s, pl.ds(x * 8 + y, 1)] for x in range(8)], axis=0)
                py[e][sy, s] = pack_cols(face)
            return carry

        lax.fori_loop(0, 4, one, 0)
        for copy in copies(e):
            copy.start()

    def at(b, o, which=0):
        return idx[(b * 27 + o) * 3 + which]

    def put(z, p, xs, ys, values):
        both = jnp.concatenate(values, axis=1).astype(BF16)
        zp[z, p, xs, ys] = both.reshape(zp[z, p, xs, ys].shape)

    def inner(z):
        def one(t, carry):
            p, x = t // 8, t % 8
            values = []
            for s in range(2):
                b = 2 * p + s
                take = [field[at(b, 12 + j), pl.ds(x * 8, 8)] for j in range(3)]
                values.append(triple(*take))
            put(z, p, pl.ds(x + 1, 1), pl.ds(1, 8), values)
            return carry

        lax.fori_loop(0, 16, one, 0)

    def halo(z, e):
        def one(p, carry):
            for sx in range(2):
                ox, cell = 2 * sx - 1, 9 * sx
                values = []
                for s in range(2):
                    o = 9 * (ox + 1) + 3
                    take = [unpack_cols(px[e][sx, at(2 * p + s, o + j)]) for j in range(3)]
                    values.append(triple(*take))
                put(z, p, pl.ds(cell, 1), pl.ds(1, 8), values)
            for sy in range(2):
                oy, cell = 2 * sy - 1, 9 * sy
                values = []
                for s in range(2):
                    o = 9 + 3 * (oy + 1)
                    take = [unpack_cols(py[e][sy, at(2 * p + s, o + j)]) for j in range(3)]
                    values.append(triple(*take))
                put(z, p, pl.ds(1, 8), pl.ds(cell, 1), values)
            for sx in range(2):
                for sy in range(2):
                    values = []
                    for s in range(2):
                        take = []
                        for j in range(3):
                            o = 18 * sx + 6 * sy + j
                            b = 2 * p + s
                            ix, iy, iq = at(b, o), at(b, o, 1), at(b, o, 2)
                            if sy == 0:
                                from_x = swap_halves(px[e][sx, ix, 16:32].astype(F32)[8:16])
                            else:
                                from_x = px[e][sx, ix, 0:16].astype(F32)[0:8]
                            if sx == 0:
                                from_y = swap_halves(py[e][sy, iy, 16:32].astype(F32)[8:16])
                            else:
                                from_y = py[e][sy, iy, 0:16].astype(F32)[0:8]
                            total = from_x + from_y + pd[e][sx * 2 + sy, iq]
                            take.append(total.reshape(1, 8, 128))
                        values.append(triple(*take))
                    put(z, p, pl.ds(9 * sx, 1), pl.ds(9 * sy, 1), values)
            return carry

        lax.fori_loop(0, 2, one, 0)

    def conv(z, p, forward):
        stack = jnp.concatenate(
            [zp[z, p, :, dy:dy + 8].reshape(1280, 256) for dy in range(3)], axis=1
        )
        if forward:
            acc = lax.dot_general(
                stack, wf[...], (((1,), (1,)), ((), ())), preferred_element_type=F32
            )
        else:
            acc = jnp.dot(stack, wb[...], preferred_element_type=F32)
        acc = acc.reshape(10, 8, 16, 256)
        low, high = acc[..., 0:128], acc[..., 128:256]
        return low[0:8] + swap_halves(low[1:9]) + high[2:10]

    def to_field(p, value):
        value = value.reshape(64, 2, 8, 128)
        for s in range(2):
            field[2 * p + s] = value[:, s]

    def correlate(layer):
        for dy in range(3):
            total = jnp.zeros((256, 256), F32)
            for p in range(2):
                z = zp[layer, p, :, dy:dy + 8].reshape(1280, 256)
                total = total + jnp.dot(d3t[p], z, preferred_element_type=F32)
            raw[layer, dy] = total

    def spread(p, delta):
        lane = lane_iota((10, 8, 16, 128))
        zeros = jnp.zeros((2, 8, 16, 128), F32)
        wide = jnp.concatenate([zeros, delta, zeros], axis=0)
        first = jnp.where(lane < 64, wide[2:12], swap_halves(wide[1:11]))
        second = jnp.where(lane < 64, wide[0:10], 0.0)
        both = jnp.concatenate([first, second], axis=3).reshape(1280, 256)
        d3t[p] = both.T.astype(BF16)

    load_field(feat)
    pl.semaphore_wait(barrier, len(DIRS))

    for layer in range(LAYERS):
        faces_out(layer)
        inner(layer)
        build_wf(layer)
        for copy in copies(layer):
            copy.wait()
        halo(layer, layer)

        def forward(p, carry):
            value = conv(layer, p, True)
            pre[layer, p] = value
            act = (value * sigmoid(value)).astype(BF16).astype(F32)
            to_field(p, act)
            return carry

        lax.fori_loop(0, 2, forward, 0)

    def store_out(s, carry):
        out[s] = field[s].reshape(512, 128).T[0:64].astype(BF16)
        return carry

    lax.fori_loop(0, 4, store_out, 0)

    def make_delta(layer, p, grad):
        v = pre[layer, p]
        s = sigmoid(v)
        delta = (grad * (s * (1.0 + v * (1.0 - s)))).astype(BF16).astype(F32)
        spread(p, delta)
        to_field(p, delta)

    load_field(cot)

    def top(p, carry):
        grad = jnp.concatenate(
            [field[2 * p + s].reshape(64, 1, 8, 128) for s in range(2)], axis=1
        )
        make_delta(2, p, grad.reshape(8, 8, 16, 128))
        return carry

    lax.fori_loop(0, 2, top, 0)
    for layer in (2, 1):
        e = 5 - layer
        faces_out(e)
        inner(3)
        build_wb(layer)
        correlate(layer)
        for copy in copies(e):
            copy.wait()
        halo(3, e)

        def backward(p, carry):
            grad = conv(3, p, False).astype(BF16).astype(F32)
            make_delta(layer - 1, p, grad)
            return carry

        lax.fori_loop(0, 2, backward, 0)
    correlate(0)


def local(features, weights, cotangent, neighbours):
    rows, cols = lax.axis_size("tx"), lax.axis_size("ty")
    vmem = pl.BlockSpec(memory_space=pltpu.VMEM)
    out, raw = pl.pallas_call(
        functools.partial(kernel, rows, cols),
        out_shape=(
            jax.ShapeDtypeStruct((4, 64, 512), BF16),
            jax.ShapeDtypeStruct((LAYERS, 3, 256, 256), F32),
        ),
        in_specs=[vmem, vmem, vmem, pl.BlockSpec(memory_space=pltpu.SMEM)],
        out_specs=(vmem, vmem),
        scratch_shapes=[
            pltpu.SMEM((4 * 27 * 3,), jnp.int32),
            pltpu.VMEM((5, 64, 8, 128), F32),
            pltpu.VMEM((4, 2, 10, 10, 16, 256), BF16),
            pltpu.VMEM((3, 2, 8, 8, 16, 128), F32),
            pltpu.VMEM((256, 768), BF16),
            pltpu.VMEM((768, 256), BF16),
            pltpu.VMEM((2, 256, 1280), BF16),
            pltpu.SemaphoreType.DMA((5, 8)),
            pltpu.SemaphoreType.DMA((5, 8)),
        ]
        + [pltpu.VMEM((2, 9, 32, 128), BF16)] * 10
        + [pltpu.VMEM((4, 5, 8, 128), F32)] * 5
        + [pltpu.VMEM((4, 4, 8, 128), F32)] * 5,
        compiler_params=pltpu.CompilerParams(
            collective_id=0, has_side_effects=True, vmem_limit_bytes=56 * 1024 * 1024
        ),
    )(features, weights, cotangent, neighbours)
    raw = raw[:, :, :192, :192].reshape(LAYERS, 3, 3, 64, 3, 64)
    raw = jnp.transpose(raw, (0, 2, 1, 4, 3, 5)).reshape(LAYERS, 27, 64, 64)
    raw = lax.psum(raw, ("tx", "ty"))
    return out, raw * (1.0 / math.sqrt(4 * rows * cols * BLK**3))


def solution(mesh):
    placed = (P(("tx", "ty"), None, None), P(), P(("tx", "ty"), None, None), P(("tx", "ty"), None))
    return jax.shard_map(
        local,
        mesh=mesh,
        in_specs=placed,
        out_specs=(P(("tx", "ty"), None, None), P()),
        check_vma=False,
    )
```

```python
import functools
import math

import jax
import jax.numpy as jnp
from jax import lax
from jax.experimental import pallas as pl
from jax.experimental.pallas import tpu as pltpu
from jax.sharding import PartitionSpec as P

BLK = 8
LAYERS = 3
F32 = jnp.float32
BF16 = jnp.bfloat16
MESH = pl.DeviceIdType.MESH
DIRS = [(-1, 0), (1, 0), (0, -1), (0, 1), (-1, -1), (-1, 1), (1, -1), (1, 1)]
UNIT_KERNELS = (
    [(9 * dx + 3 * dy, 9 * dx + 3 * dy + 1) for dy in range(3) for dx in range(3)]
    + [(9 * dx + 2, 9 * dx + 5) for dx in range(3)]
    + [(8, 17), (26,)]
)
UNITS = len(UNIT_KERNELS)


def lane_iota(shape):
    return lax.broadcasted_iota(jnp.int32, shape, len(shape) - 1)


def swap_halves(value):
    return pltpu.roll(value, 64, len(value.shape) - 1)


def pack_cols(face):
    low, high = face[0:4], face[4:8]
    packed = jnp.where(lane_iota(low.shape) < 64, low, swap_halves(high))
    return packed.reshape(32, 128).astype(BF16)


def unpack_cols(packed):
    wide = packed.astype(F32).reshape(4, 8, 128)
    return jnp.concatenate([wide, swap_halves(wide)], axis=0)


def triple(below, here, above):
    z = lax.broadcasted_iota(jnp.int32, here.shape, 1)
    lane = lane_iota(here.shape)
    down = pltpu.roll(jnp.where(z == 7, below, here), 1, 1)
    up = pltpu.roll(jnp.where(z == 0, above, here), 7, 1)
    first = jnp.where(lane < 64, down, swap_halves(here))
    second = jnp.where(lane < 64, up, 0.0)
    return jnp.concatenate([first, second], axis=2)


def sigmoid(value):
    return 1.0 / (1.0 + jnp.exp(-value))


def kernel(
    rows, cols, scale, feat, w, cot, nbr, out, grads,
    idx, field, zp, pre, wf, wb, d3t, raw, sums, send_sem, recv_sem, sum_send, sum_recv, *pools,
):
    px, py, pd, sd = pools[0:5], pools[5:10], pools[10:15], pools[15:20]
    mine, from_cols, from_rows, shares, full = (pools[20 + 3 * n:23 + 3 * n] for n in range(5))
    r, c = lax.axis_index("tx"), lax.axis_index("ty")

    def peer(dr, dc):
        return (lax.rem(r + dr + rows, rows), lax.rem(c + dc + cols, cols))

    barrier = pltpu.get_barrier_semaphore()
    partners = sorted(
        {(dr % rows, dc % cols) for dr, dc in DIRS}
        | {(k, 0) for k in range(1, rows)}
        | {(0, k) for k in range(1, cols)}
    )
    for dr, dc in partners:
        pl.semaphore_signal(barrier, inc=1, device_id=peer(dr, dc), device_id_type=MESH)

    def fill_idx(b, carry):
        for o in range(27):
            ox, oy = o // 9 - 1, o // 3 % 3 - 1
            n = nbr[b, o]
            there = n >= 0
            n = jnp.maximum(n, 0)
            slot = n & 3
            dev = n >> 2
            same_r, same_c = (dev // cols) == r, (dev % cols) == c
            base = (b * 27 + o) * 3
            if ox == 0 and oy == 0:
                idx[base] = jnp.where(there, slot, 4)
            elif oy == 0:
                idx[base] = jnp.where(there, slot + jnp.where(same_r, 0, 4), 8)
            elif ox == 0:
                idx[base] = jnp.where(there, slot + jnp.where(same_c, 0, 4), 8)
            else:
                idx[base] = jnp.where(there & same_c, slot + jnp.where(same_r, 0, 4), 8)
                idx[base + 1] = jnp.where(
                    there & same_r & jnp.logical_not(same_c), slot + 4, 8
                )
                idx[base + 2] = jnp.where(
                    there & jnp.logical_not(same_r) & jnp.logical_not(same_c), slot, 4
                )
        return carry

    lax.fori_loop(0, 4, fill_idx, 0)

    field[4] = jnp.zeros((64, 8, 128), F32)
    for e in range(5):
        for s in range(2):
            px[e][s, 8] = jnp.zeros((32, 128), BF16)
            py[e][s, 8] = jnp.zeros((32, 128), BF16)
        for q in range(4):
            pd[e][q, 4] = jnp.zeros((8, 128), F32)

    def load_field(source):
        def one(s, carry):
            wide = source[s].astype(F32)
            wide = jnp.concatenate([wide, jnp.zeros((64, 512), F32)], axis=0)
            field[s] = wide.T.reshape(64, 8, 128)
            return carry

        lax.fori_loop(0, 4, one, 0)

    def build_wf(layer):
        for dx in range(3):
            rows_here = []
            for dy in range(3):
                for dz in range(3):
                    rows_here.append(w[layer, 9 * dx + 3 * dy + dz])
                rows_here.append(jnp.zeros((64, 64), BF16))
            wf[dx * 64:(dx + 1) * 64, :] = jnp.concatenate(rows_here, axis=1)
        wf[192:256, :] = jnp.zeros((64, 768), BF16)

    def build_wb(layer):
        for dy in range(3):
            for dz in range(3):
                row = dy * 256 + dz * 64
                parts = [w[layer, 26 - (9 * dx + 3 * dy + dz)] for dx in range(3)]
                parts.append(jnp.zeros((64, 64), BF16))
                wb[row:row + 64, :] = jnp.concatenate(parts, axis=1)
            wb[dy * 256 + 192:dy * 256 + 256, :] = jnp.zeros((64, 256), BF16)

    def copies(e):
        made = []
        for k, (dr, dc) in enumerate(DIRS):
            if dc == 0:
                s = 0 if dr > 0 else 1
                src, dst = px[e].at[s, pl.ds(0, 4)], px[e].at[s, pl.ds(4, 4)]
            elif dr == 0:
                s = 0 if dc > 0 else 1
                src, dst = py[e].at[s, pl.ds(0, 4)], py[e].at[s, pl.ds(4, 4)]
            else:
                q = (0 if dr > 0 else 1) * 2 + (0 if dc > 0 else 1)
                src, dst = sd[e].at[q], pd[e].at[q, pl.ds(0, 4)]
            made.append(
                pltpu.make_async_remote_copy(
                    src_ref=src, dst_ref=dst, send_sem=send_sem.at[e, k],
                    recv_sem=recv_sem.at[e, k], device_id=peer(dr, dc), device_id_type=MESH,
                )
            )
        return made

    def faces_out(e):
        def one(s, carry):
            for sx in range(2):
                x = 7 if sx == 0 else 0
                face = field[s, pl.ds(x * 8, 8)]
                px[e][sx, s] = pack_cols(face)
                for sy in range(2):
                    y = 7 if sy == 0 else 0
                    sd[e][sx * 2 + sy, s] = face[y]
            for sy in range(2):
                y = 7 if sy == 0 else 0
                face = jnp.concatenate([field[s, pl.ds(x * 8 + y, 1)] for x in range(8)], axis=0)
                py[e][sy, s] = pack_cols(face)
            return carry

        lax.fori_loop(0, 4, one, 0)
        for copy in copies(e):
            copy.start()

    def at(b, o, which=0):
        return idx[(b * 27 + o) * 3 + which]

    def put(z, p, xs, ys, values):
        both = jnp.concatenate(values, axis=1).astype(BF16)
        zp[z, p, xs, ys] = both.reshape(zp[z, p, xs, ys].shape)

    def inner(z):
        def one(t, carry):
            p, x = t // 8, t % 8
            values = []
            for s in range(2):
                b = 2 * p + s
                take = [field[at(b, 12 + j), pl.ds(x * 8, 8)] for j in range(3)]
                values.append(triple(*take))
            put(z, p, pl.ds(x + 1, 1), pl.ds(1, 8), values)
            return carry

        lax.fori_loop(0, 16, one, 0)

    def halo(z, e):
        def one(p, carry):
            for sx in range(2):
                ox, cell = 2 * sx - 1, 9 * sx
                values = []
                for s in range(2):
                    o = 9 * (ox + 1) + 3
                    take = [unpack_cols(px[e][sx, at(2 * p + s, o + j)]) for j in range(3)]
                    values.append(triple(*take))
                put(z, p, pl.ds(cell, 1), pl.ds(1, 8), values)
            for sy in range(2):
                oy, cell = 2 * sy - 1, 9 * sy
                values = []
                for s in range(2):
                    o = 9 + 3 * (oy + 1)
                    take = [unpack_cols(py[e][sy, at(2 * p + s, o + j)]) for j in range(3)]
                    values.append(triple(*take))
                put(z, p, pl.ds(1, 8), pl.ds(cell, 1), values)
            for sx in range(2):
                for sy in range(2):
                    values = []
                    for s in range(2):
                        take = []
                        for j in range(3):
                            o = 18 * sx + 6 * sy + j
                            b = 2 * p + s
                            ix, iy, iq = at(b, o), at(b, o, 1), at(b, o, 2)
                            if sy == 0:
                                from_x = swap_halves(px[e][sx, ix, 16:32].astype(F32)[8:16])
                            else:
                                from_x = px[e][sx, ix, 0:16].astype(F32)[0:8]
                            if sx == 0:
                                from_y = swap_halves(py[e][sy, iy, 16:32].astype(F32)[8:16])
                            else:
                                from_y = py[e][sy, iy, 0:16].astype(F32)[0:8]
                            total = from_x + from_y + pd[e][sx * 2 + sy, iq]
                            take.append(total.reshape(1, 8, 128))
                        values.append(triple(*take))
                    put(z, p, pl.ds(9 * sx, 1), pl.ds(9 * sy, 1), values)
            return carry

        lax.fori_loop(0, 2, one, 0)

    def conv(z, p, forward):
        stack = jnp.concatenate(
            [zp[z, p, :, dy:dy + 8].reshape(1280, 256) for dy in range(3)], axis=1
        )
        if forward:
            acc = lax.dot_general(
                stack, wf[...], (((1,), (1,)), ((), ())), preferred_element_type=F32
            )
        else:
            acc = jnp.dot(stack, wb[...], preferred_element_type=F32)
        acc = acc.reshape(10, 8, 16, 256)
        low, high = acc[..., 0:128], acc[..., 128:256]
        return low[0:8] + swap_halves(low[1:9]) + high[2:10]

    def to_field(p, value):
        value = value.reshape(64, 2, 8, 128)
        for s in range(2):
            field[2 * p + s] = value[:, s]

    def correlate(layer):
        for dy in range(3):
            total = jnp.zeros((256, 256), F32)
            for p in range(2):
                z = zp[layer, p, :, dy:dy + 8].reshape(1280, 256)
                total = total + jnp.dot(d3t[p], z, preferred_element_type=F32)
            raw[dy] = total
        lane = lane_iota((64, 128))
        for dx in range(3):
            at_dx = slice(dx * 64, dx * 64 + 64)
            for dy in range(3):
                mine[layer][dy * 3 + dx] = raw[dy, at_dx, 0:128].astype(BF16)
            pair = jnp.where(
                lane < 64, raw[0, at_dx, 128:256], swap_halves(raw[1, at_dx, 128:256])
            )
            mine[layer][9 + dx] = pair.astype(BF16)
        pair = jnp.where(lane < 64, raw[2, 0:64, 128:256], swap_halves(raw[2, 64:128, 128:256]))
        mine[layer][12] = pair.astype(BF16)
        mine[layer][13] = raw[2, 128:192, 128:256].astype(BF16)

    has_unit = c < UNITS

    def wait_bytes(ref, count, sem):
        part = ref.at[pl.ds(0, count)]
        pltpu.make_async_copy(part, part, sem).wait()

    def sum_copy(layer, phase, src, dst, device):
        return pltpu.make_async_remote_copy(
            src_ref=src, dst_ref=dst, send_sem=sum_send.at[layer, phase],
            recv_sem=sum_recv.at[layer, phase], device_id=device, device_id_type=MESH,
        )

    def over(size, body):
        def one(k, carry):
            body(k)
            return carry

        lax.fori_loop(1, size, one, 0)

    def sum_0(layer):
        def send(k):
            to = lax.rem(c + k, cols)

            @pl.when(to < UNITS)
            def _():
                sum_copy(layer, 0, mine[layer].at[to], from_cols[layer].at[c], (r, to)).start()

        over(cols, send)

    def sum_1(layer):
        @pl.when(has_unit)
        def _():
            wait_bytes(from_cols[layer], cols - 1, sum_recv.at[layer, 0])
            from_cols[layer][c] = mine[layer][c]
            total = from_cols[layer][0].astype(F32)
            for k in range(1, cols):
                total = total + from_cols[layer][k].astype(F32)
            sums[layer] = total.reshape(8, 8, 128)

            def send(k):
                to = lax.rem(r + k, rows)
                sum_copy(
                    layer, 1, sums.at[layer, to], from_rows[layer].at[r], (to, c)
                ).start()

            over(rows, send)

    def sum_2(layer):
        @pl.when(has_unit)
        def _():
            wait_bytes(from_rows[layer], rows - 1, sum_recv.at[layer, 1])
            from_rows[layer][r] = sums[layer, r]
            total = from_rows[layer][0]
            for k in range(1, rows):
                total = total + from_rows[layer][k]
            shares[layer][r] = total * scale

            def send(k):
                to = lax.rem(r + k, rows)
                sum_copy(
                    layer, 2, shares[layer].at[r], shares[layer].at[r], (to, c)
                ).start()

            over(rows, send)

    def sum_3(layer):
        @pl.when(has_unit)
        def _():
            wait_bytes(shares[layer], rows - 1, sum_recv.at[layer, 2])
            full[layer][c] = shares[layer][...].reshape(64, 128).astype(BF16)

            def send(k):
                to = lax.rem(c + k, cols)
                sum_copy(layer, 3, full[layer].at[c], full[layer].at[c], (r, to)).start()

            over(cols, send)

    def sum_4(layer):
        @pl.when(has_unit)
        def _():
            wait_bytes(full[layer], UNITS - 1, sum_recv.at[layer, 3])

        @pl.when(jnp.logical_not(has_unit))
        def _():
            wait_bytes(full[layer], UNITS, sum_recv.at[layer, 3])

        for unit, pair in enumerate(UNIT_KERNELS):
            value = full[layer][unit].astype(F32)
            grads[layer, pair[0]] = value[:, 0:64]
            if len(pair) > 1:
                grads[layer, pair[1]] = swap_halves(value)[:, 0:64]

    def sum_end(layer):
        @pl.when(has_unit)
        def _():
            wait_bytes(mine[layer], UNITS - 1, sum_send.at[layer, 0])
            wait_bytes(from_rows[layer], rows - 1, sum_send.at[layer, 1])
            wait_bytes(shares[layer], rows - 1, sum_send.at[layer, 2])
            wait_bytes(from_cols[layer], cols - 1, sum_send.at[layer, 3])

        @pl.when(jnp.logical_not(has_unit))
        def _():
            wait_bytes(mine[layer], UNITS, sum_send.at[layer, 0])

    def spread(p, delta):
        lane = lane_iota((10, 8, 16, 128))
        zeros = jnp.zeros((2, 8, 16, 128), F32)
        wide = jnp.concatenate([zeros, delta, zeros], axis=0)
        first = jnp.where(lane < 64, wide[2:12], swap_halves(wide[1:11]))
        second = jnp.where(lane < 64, wide[0:10], 0.0)
        both = jnp.concatenate([first, second], axis=3).reshape(1280, 256)
        d3t[p] = both.T.astype(BF16)

    load_field(feat)
    pl.semaphore_wait(barrier, len(partners))

    for layer in range(LAYERS):
        faces_out(layer)
        inner(layer)
        build_wf(layer)
        for copy in copies(layer):
            copy.wait()
        halo(layer, layer)

        def forward(p, carry):
            value = conv(layer, p, True)
            pre[layer, p] = value
            act = (value * sigmoid(value)).astype(BF16).astype(F32)
            to_field(p, act)
            return carry

        lax.fori_loop(0, 2, forward, 0)

    def store_out(s, carry):
        out[s] = field[s].reshape(512, 128).T[0:64].astype(BF16)
        return carry

    lax.fori_loop(0, 4, store_out, 0)

    def make_delta(layer, p, grad):
        v = pre[layer, p]
        s = sigmoid(v)
        delta = (grad * (s * (1.0 + v * (1.0 - s)))).astype(BF16).astype(F32)
        spread(p, delta)
        to_field(p, delta)

    load_field(cot)

    def top(p, carry):
        grad = jnp.concatenate(
            [field[2 * p + s].reshape(64, 1, 8, 128) for s in range(2)], axis=1
        )
        make_delta(2, p, grad.reshape(8, 8, 16, 128))
        return carry

    lax.fori_loop(0, 2, top, 0)
    for layer in (2, 1):
        e = 5 - layer
        faces_out(e)
        inner(3)
        build_wb(layer)
        correlate(layer)
        sum_0(layer)
        if layer == 1:
            sum_1(2)
        for copy in copies(e):
            copy.wait()
        halo(3, e)

        def backward(p, carry):
            grad = conv(3, p, False).astype(BF16).astype(F32)
            make_delta(layer - 1, p, grad)
            return carry

        lax.fori_loop(0, 2, backward, 0)
    correlate(0)
    sum_0(0)
    sum_2(2)
    sum_1(1)
    sum_1(0)
    sum_3(2)
    sum_2(1)
    sum_2(0)
    sum_4(2)
    sum_3(1)
    sum_3(0)
    sum_4(1)
    sum_4(0)
    for layer in range(LAYERS):
        sum_end(layer)


def local(features, weights, cotangent, neighbours):
    rows, cols = lax.axis_size("tx"), lax.axis_size("ty")
    vmem = pl.BlockSpec(memory_space=pltpu.VMEM)
    return pl.pallas_call(
        functools.partial(kernel, rows, cols, 1.0 / math.sqrt(4 * rows * cols * BLK**3)),
        out_shape=(
            jax.ShapeDtypeStruct((4, 64, 512), BF16),
            jax.ShapeDtypeStruct((LAYERS, 27, 64, 64), F32),
        ),
        in_specs=[vmem, vmem, vmem, pl.BlockSpec(memory_space=pltpu.SMEM)],
        out_specs=(vmem, vmem),
        scratch_shapes=[
            pltpu.SMEM((4 * 27 * 3,), jnp.int32),
            pltpu.VMEM((5, 64, 8, 128), F32),
            pltpu.VMEM((4, 2, 10, 10, 16, 256), BF16),
            pltpu.VMEM((3, 2, 8, 8, 16, 128), F32),
            pltpu.VMEM((256, 768), BF16),
            pltpu.VMEM((768, 256), BF16),
            pltpu.VMEM((2, 256, 1280), BF16),
            pltpu.VMEM((3, 256, 256), F32),
            pltpu.VMEM((LAYERS, 8, 8, 128), F32),
            pltpu.SemaphoreType.DMA((5, 8)),
            pltpu.SemaphoreType.DMA((5, 8)),
            pltpu.SemaphoreType.DMA((LAYERS, 4)),
            pltpu.SemaphoreType.DMA((LAYERS, 4)),
        ]
        + [pltpu.VMEM((2, 9, 32, 128), BF16)] * 10
        + [pltpu.VMEM((4, 5, 8, 128), F32)] * 5
        + [pltpu.VMEM((4, 4, 8, 128), F32)] * 5
        + [pltpu.VMEM((UNITS, 64, 128), BF16)] * LAYERS
        + [pltpu.VMEM((cols, 64, 128), BF16)] * LAYERS
        + [pltpu.VMEM((rows, 8, 128), F32)] * LAYERS
        + [pltpu.VMEM((rows, 8, 128), F32)] * LAYERS
        + [pltpu.VMEM((UNITS, 64, 128), BF16)] * LAYERS,
        compiler_params=pltpu.CompilerParams(
            collective_id=0, has_side_effects=True, vmem_limit_bytes=56 * 1024 * 1024
        ),
    )(features, weights, cotangent, neighbours)


def solution(mesh):
    placed = (P(("tx", "ty"), None, None), P(), P(("tx", "ty"), None, None), P(("tx", "ty"), None))
    return jax.shard_map(
        local,
        mesh=mesh,
        in_specs=placed,
        out_specs=(P(("tx", "ty"), None, None), P()),
        check_vma=False,
    )
```

```python
import functools
import math

import jax
import jax.numpy as jnp
from jax import lax
from jax.experimental import pallas as pl
from jax.experimental.pallas import tpu as pltpu
from jax.sharding import PartitionSpec as P

BLK = 8
LAYERS = 3
F32 = jnp.float32
BF16 = jnp.bfloat16
MESH = pl.DeviceIdType.MESH
DIRS = [(-1, -1), (-1, 1), (1, -1), (1, 1), (0, -1), (0, 1), (-1, 0), (1, 0)]
UNIT_KERNELS = (
    [(9 * dx + 3 * dy, 9 * dx + 3 * dy + 1) for dy in range(3) for dx in range(3)]
    + [(9 * dx + 2, 9 * dx + 5) for dx in range(3)]
    + [(8, 17), (26,)]
)
UNITS = len(UNIT_KERNELS)


def lane_iota(shape):
    return lax.broadcasted_iota(jnp.int32, shape, len(shape) - 1)


def swap_halves(value):
    return pltpu.roll(value, 64, len(value.shape) - 1)


def pack_cols(face):
    low, high = face[0:4], face[4:8]
    packed = jnp.where(lane_iota(low.shape) < 64, low, swap_halves(high))
    return packed.reshape(32, 128).astype(BF16)


def unpack_cols(packed):
    wide = packed.astype(F32).reshape(4, 8, 128)
    return jnp.concatenate([wide, swap_halves(wide)], axis=0)


def triple(below, here, above):
    z = lax.broadcasted_iota(jnp.int32, here.shape, 1)
    lane = lane_iota(here.shape)
    down = pltpu.roll(jnp.where(z == 7, below, here), 1, 1)
    up = pltpu.roll(jnp.where(z == 0, above, here), 7, 1)
    first = jnp.where(lane < 64, down, swap_halves(here))
    second = jnp.where(lane < 64, up, 0.0)
    return jnp.concatenate([first, second], axis=2)


def sigmoid(value):
    return 1.0 / (1.0 + jnp.exp(-value))


def kernel(
    rows, cols, scale, feat, w, cot, nbr, out, grads,
    idx, field, zp, pre, wf, wb, d3t, raw, part, corner,
    send_sem, recv_sem, sum_send, sum_recv, *pools,
):
    px, py, pd, sd = pools[0:5], pools[5:10], pools[10:15], pools[15:20]
    mine, from_cols, from_rows, full = (pools[20 + 3 * n:23 + 3 * n] for n in range(4))
    r, c = lax.axis_index("tx"), lax.axis_index("ty")

    def peer(dr, dc):
        return (lax.rem(r + dr + rows, rows), lax.rem(c + dc + cols, cols))

    def inside(dr, dc):
        return (r + dr >= 0) & (r + dr < rows) & (c + dc >= 0) & (c + dc < cols)

    barrier = pltpu.get_barrier_semaphore()
    greeted = rows - 1 + cols - 1
    for dr, dc in DIRS[:4]:
        greeted = greeted + inside(dr, dc).astype(jnp.int32)

        @pl.when(inside(dr, dc))
        def _():
            pl.semaphore_signal(barrier, inc=1, device_id=peer(dr, dc), device_id_type=MESH)

    for dr, dc in [(0, k) for k in range(1, cols)] + [(k, 0) for k in range(1, rows)]:
        pl.semaphore_signal(barrier, inc=1, device_id=peer(dr, dc), device_id_type=MESH)

    def fill_idx(b, carry):
        for o in range(27):
            ox, oy = o // 9 - 1, o // 3 % 3 - 1
            n = nbr[b, o]
            there = n >= 0
            n = jnp.maximum(n, 0)
            slot = n & 3
            dev = n >> 2
            same_r, same_c = (dev // cols) == r, (dev % cols) == c
            base = (b * 27 + o) * 3
            if ox == 0 and oy == 0:
                idx[base] = jnp.where(there, slot, 4)
            elif oy == 0:
                idx[base] = jnp.where(there, slot + jnp.where(same_r, 0, 4), 8)
            elif ox == 0:
                idx[base] = jnp.where(there, slot + jnp.where(same_c, 0, 4), 8)
            else:
                idx[base] = jnp.where(there & same_c, slot + jnp.where(same_r, 0, 4), 8)
                idx[base + 1] = jnp.where(
                    there & same_r & jnp.logical_not(same_c), slot + 4, 8
                )
                idx[base + 2] = jnp.where(
                    there & jnp.logical_not(same_r) & jnp.logical_not(same_c), slot, 4
                )
        return carry

    lax.fori_loop(0, 4, fill_idx, 0)

    field[4] = jnp.zeros((64, 8, 128), F32)
    for e in range(5):
        for s in range(2):
            px[e][s, 8] = jnp.zeros((32, 128), BF16)
            py[e][s, 8] = jnp.zeros((32, 128), BF16)
        for p in range(2):
            for y in (0, 9):
                zp[e, p, 1:9, y] = jnp.zeros((8, 16, 256), BF16)
    for q in range(4):
        corner[q, 4] = jnp.zeros((8, 128), F32)

    def load_field(source):
        def one(s, carry):
            wide = source[s].astype(F32)
            wide = jnp.concatenate([wide, jnp.zeros((64, 512), F32)], axis=0)
            field[s] = wide.T.reshape(64, 8, 128)
            return carry

        lax.fori_loop(0, 4, one, 0)

    def build_wf(layer):
        for dx in range(3):
            rows_here = []
            for dy in range(3):
                for dz in range(3):
                    rows_here.append(w[layer, 9 * dx + 3 * dy + dz])
                rows_here.append(jnp.zeros((64, 64), BF16))
            wf[layer, dx * 64:(dx + 1) * 64, :] = jnp.concatenate(rows_here, axis=1)
        wf[layer, 192:256, :] = jnp.zeros((64, 768), BF16)

    def build_wb(layer):
        for dy in range(3):
            for dz in range(3):
                row = dy * 256 + dz * 64
                parts = [w[layer, 26 - (9 * dx + 3 * dy + dz)] for dx in range(3)]
                parts.append(jnp.zeros((64, 64), BF16))
                wb[layer - 1, row:row + 64, :] = jnp.concatenate(parts, axis=1)
            wb[layer - 1, dy * 256 + 192:dy * 256 + 256, :] = jnp.zeros((64, 256), BF16)

    def copies(e):
        made = []
        for k, (dr, dc) in enumerate(DIRS):
            if dc == 0:
                s = 0 if dr > 0 else 1
                src, dst = px[e].at[s, pl.ds(0, 4)], px[e].at[s, pl.ds(4, 4)]
            elif dr == 0:
                s = 0 if dc > 0 else 1
                src, dst = py[e].at[s, pl.ds(0, 4)], py[e].at[s, pl.ds(4, 4)]
            else:
                q = (0 if dr > 0 else 1) * 2 + (0 if dc > 0 else 1)
                src, dst = sd[e].at[q], pd[e].at[q]
            copy = (
                pltpu.make_async_remote_copy(
                    src_ref=src, dst_ref=dst, send_sem=send_sem.at[e, k],
                    recv_sem=recv_sem.at[e, k], device_id=peer(dr, dc), device_id_type=MESH,
                )
            )
            made.append((inside(dr, dc), inside(-dr, -dc), copy))
        return made

    def arrive(e):
        for sends, receives, copy in copies(e):
            pl.when(sends)(copy.wait_send)
            pl.when(receives)(copy.wait_recv)

    def faces_out(e):
        def one(s, carry):
            for sx in range(2):
                x = 7 if sx == 0 else 0
                face = field[s, pl.ds(x * 8, 8)]
                px[e][sx, s] = pack_cols(face)
                for sy in range(2):
                    y = 7 if sy == 0 else 0
                    corner[sx * 2 + sy, s] = face[y]
            for sy in range(2):
                y = 7 if sy == 0 else 0
                face = jnp.concatenate([field[s, pl.ds(x * 8 + y, 1)] for x in range(8)], axis=0)
                py[e][sy, s] = pack_cols(face)
            return carry

        lax.fori_loop(0, 4, one, 0)
        lane = lane_iota((16, 128))
        for q in range(4):
            low = corner[q, 0:2].reshape(16, 128)
            high = corner[q, 2:4].reshape(16, 128)
            sd[e][q] = jnp.where(lane < 64, low, swap_halves(high)).astype(BF16)

    def send_faces(e):
        for sends, _, copy in copies(e):
            pl.when(sends)(copy.start)

    def at(b, o, which=0):
        return idx[(b * 27 + o) * 3 + which]

    def put(z, p, xs, ys, values):
        both = jnp.concatenate(values, axis=1).astype(BF16)
        zp[z, p, xs, ys] = both.reshape(zp[z, p, xs, ys].shape)

    def inner(z):
        def one(t, carry):
            p, x = t // 8, t % 8
            values = []
            for s in range(2):
                b = 2 * p + s
                take = [field[at(b, 12 + j), pl.ds(x * 8, 8)] for j in range(3)]
                values.append(triple(*take))
            put(z, p, pl.ds(x + 1, 1), pl.ds(1, 8), values)
            return carry

        lax.fori_loop(0, 16, one, 0)

    def halo(z, e):
        for q in range(4):
            wide = pd[e][q].astype(F32)
            corner[q, 0:2] = wide.reshape(2, 8, 128)
            corner[q, 2:4] = swap_halves(wide).reshape(2, 8, 128)

        def one(p, carry):
            for sx in range(2):
                ox, cell = 2 * sx - 1, 9 * sx
                values = []
                for s in range(2):
                    o = 9 * (ox + 1) + 3
                    take = [unpack_cols(px[e][sx, at(2 * p + s, o + j)]) for j in range(3)]
                    values.append(triple(*take))
                put(z, p, pl.ds(cell, 1), pl.ds(1, 8), values)
            for sy in range(2):
                oy, cell = 2 * sy - 1, 9 * sy
                values = []
                for s in range(2):
                    o = 9 + 3 * (oy + 1)
                    take = [unpack_cols(py[e][sy, at(2 * p + s, o + j)]) for j in range(3)]
                    values.append(triple(*take))
                put(z, p, pl.ds(1, 8), pl.ds(cell, 1), values)
            for sx in range(2):
                for sy in range(2):
                    values = []
                    for s in range(2):
                        take = []
                        for j in range(3):
                            o = 18 * sx + 6 * sy + j
                            b = 2 * p + s
                            ix, iy, iq = at(b, o), at(b, o, 1), at(b, o, 2)
                            if sy == 0:
                                from_x = swap_halves(px[e][sx, ix, 16:32].astype(F32)[8:16])
                            else:
                                from_x = px[e][sx, ix, 0:16].astype(F32)[0:8]
                            if sx == 0:
                                from_y = swap_halves(py[e][sy, iy, 16:32].astype(F32)[8:16])
                            else:
                                from_y = py[e][sy, iy, 0:16].astype(F32)[0:8]
                            total = from_x + from_y + corner[sx * 2 + sy, iq]
                            take.append(total.reshape(1, 8, 128))
                        values.append(triple(*take))
                    put(z, p, pl.ds(9 * sx, 1), pl.ds(9 * sy, 1), values)
            return carry

        lax.fori_loop(0, 2, one, 0)

    def multiply(stack, layer, forward, dy=None):
        at_dy = slice(0, 768) if dy is None else slice(dy * 256, dy * 256 + 256)
        if forward:
            return lax.dot_general(
                stack, wf[layer, :, at_dy], (((1,), (1,)), ((), ())), preferred_element_type=F32
            )
        return jnp.dot(stack, wb[layer - 1, at_dy, :], preferred_element_type=F32)

    def over_dx(acc):
        low, high = acc[..., 0:128], acc[..., 128:256]
        blank = jnp.zeros_like(low[0:1])
        left = jnp.concatenate([blank, low[0:7]], axis=0)
        right = jnp.concatenate([high[1:8], blank], axis=0)
        return left + swap_halves(low) + right

    def conv_inner(z, layer, forward):
        def one(p, carry):
            stack = jnp.concatenate(
                [zp[z, p, 1:9, dy:dy + 8].reshape(1024, 256) for dy in range(3)], axis=1
            )
            part[p] = over_dx(multiply(stack, layer, forward).reshape(8, 8, 16, 256))
            return carry

        lax.fori_loop(0, 2, one, 0)

    def conv_halo(z, layer, forward):
        planes = jnp.concatenate(
            [
                jnp.concatenate(
                    [zp[z, p, x, dy:dy + 8].reshape(128, 256) for dy in range(3)], axis=1
                )
                for x in (0, 9)
                for p in range(2)
            ],
            axis=0,
        )
        acc = multiply(planes, layer, forward).reshape(2, 2, 8, 16, 256)
        for p in range(2):
            part[p, 0] += acc[0, p, :, :, 0:128]
            part[p, 7] += acc[1, p, :, :, 128:256]
        for cell, dy, y in ((0, 0, 0), (9, 2, 7)):
            lines = jnp.concatenate(
                [zp[z, p, 1:9, cell].reshape(128, 256) for p in range(2)], axis=0
            )
            acc = multiply(lines, layer, forward, dy).reshape(2, 8, 16, 256)
            for p in range(2):
                part[p, :, y] += over_dx(acc[p])

    def to_field(p, value):
        value = value.reshape(64, 2, 8, 128)
        for s in range(2):
            field[2 * p + s] = value[:, s]

    def correlate(layer):
        for dy in range(3):
            total = jnp.zeros((256, 256), F32)
            for p in range(2):
                z = zp[layer, p, :, dy:dy + 8].reshape(1280, 256)
                total = total + jnp.dot(d3t[p], z, preferred_element_type=F32)
            raw[dy] = total
        lane = lane_iota((64, 128))
        for dx in range(3):
            at_dx = slice(dx * 64, dx * 64 + 64)
            for dy in range(3):
                mine[layer][dy * 3 + dx] = raw[dy, at_dx, 0:128].astype(BF16)
            pair = jnp.where(
                lane < 64, raw[0, at_dx, 128:256], swap_halves(raw[1, at_dx, 128:256])
            )
            mine[layer][9 + dx] = pair.astype(BF16)
        pair = jnp.where(lane < 64, raw[2, 0:64, 128:256], swap_halves(raw[2, 64:128, 128:256]))
        mine[layer][12] = pair.astype(BF16)
        mine[layer][13] = raw[2, 128:192, 128:256].astype(BF16)

    has_unit = c < UNITS

    def wait_bytes(ref, count, sem):
        part = ref.at[pl.ds(0, count)]
        pltpu.make_async_copy(part, part, sem).wait()

    def sum_copy(layer, phase, src, dst, device):
        return pltpu.make_async_remote_copy(
            src_ref=src, dst_ref=dst, send_sem=sum_send.at[layer, phase],
            recv_sem=sum_recv.at[layer, phase], device_id=device, device_id_type=MESH,
        )

    def over(size, body):
        def one(k, carry):
            body(k)
            return carry

        lax.fori_loop(1, size, one, 0)

    def sum_0(layer):
        def send(k):
            to = lax.rem(c + k, cols)

            @pl.when(to < UNITS)
            def _():
                sum_copy(layer, 0, mine[layer].at[to], from_cols[layer].at[c], (r, to)).start()

        over(cols, send)

    def sum_1(layer):
        @pl.when(has_unit)
        def _():
            wait_bytes(from_cols[layer], cols - 1, sum_recv.at[layer, 0])
            from_cols[layer][c] = mine[layer][c]
            total = from_cols[layer][0].astype(F32)
            for k in range(1, cols):
                total = total + from_cols[layer][k].astype(F32)
            from_rows[layer][r] = total.astype(BF16)

            def send(k):
                to = lax.rem(r + k, rows)
                sum_copy(
                    layer, 1, from_rows[layer].at[r], from_rows[layer].at[r], (to, c)
                ).start()

            over(rows, send)

    def sum_2(layer):
        @pl.when(has_unit)
        def _():
            wait_bytes(from_rows[layer], rows - 1, sum_recv.at[layer, 1])
            total = from_rows[layer][0].astype(F32)
            for k in range(1, rows):
                total = total + from_rows[layer][k].astype(F32)
            full[layer][c] = (total * scale).astype(BF16)

            def send(k):
                to = lax.rem(c + k, cols)
                sum_copy(layer, 2, full[layer].at[c], full[layer].at[c], (r, to)).start()

            over(cols, send)

    def sum_3(layer):
        @pl.when(has_unit)
        def _():
            wait_bytes(full[layer], UNITS - 1, sum_recv.at[layer, 2])

        @pl.when(jnp.logical_not(has_unit))
        def _():
            wait_bytes(full[layer], UNITS, sum_recv.at[layer, 2])

        grads[layer] = full[layer][...]

    def sum_end(layer):
        @pl.when(has_unit)
        def _():
            wait_bytes(mine[layer], UNITS - 1, sum_send.at[layer, 0])
            wait_bytes(from_rows[layer], rows - 1, sum_send.at[layer, 1])
            wait_bytes(from_cols[layer], cols - 1, sum_send.at[layer, 2])

        @pl.when(jnp.logical_not(has_unit))
        def _():
            wait_bytes(mine[layer], UNITS, sum_send.at[layer, 0])

    def spread(p, delta):
        lane = lane_iota((10, 8, 16, 128))
        zeros = jnp.zeros((2, 8, 16, 128), F32)
        wide = jnp.concatenate([zeros, delta, zeros], axis=0)
        first = jnp.where(lane < 64, wide[2:12], swap_halves(wide[1:11]))
        second = jnp.where(lane < 64, wide[0:10], 0.0)
        both = jnp.concatenate([first, second], axis=3).reshape(1280, 256)
        d3t[p] = both.T.astype(BF16)

    load_field(feat)
    faces_out(0)
    inner(0)
    build_wf(0)
    conv_inner(0, 0, True)
    pl.semaphore_wait(barrier, greeted)
    send_faces(0)
    for layer in (1, 2):
        build_wf(layer)
        build_wb(layer)

    for layer in range(LAYERS):
        if layer > 0:
            faces_out(layer)
            send_faces(layer)
            inner(layer)
            conv_inner(layer, layer, True)
        arrive(layer)
        halo(layer, layer)
        conv_halo(layer, layer, True)

        def forward(p, carry):
            value = part[p]
            pre[layer, p] = value
            act = (value * sigmoid(value)).astype(BF16).astype(F32)
            to_field(p, act)
            return carry

        lax.fori_loop(0, 2, forward, 0)

    def store_out(s, carry):
        out[s] = field[s].reshape(512, 128).T[0:64].astype(BF16)
        return carry

    lax.fori_loop(0, 4, store_out, 0)

    def make_delta(layer, p, grad):
        v = pre[layer, p]
        s = sigmoid(v)
        delta = (grad * (s * (1.0 + v * (1.0 - s)))).astype(BF16).astype(F32)
        part[p] = delta
        to_field(p, delta)

    def spread_all():
        def one(p, carry):
            spread(p, part[p])
            return carry

        lax.fori_loop(0, 2, one, 0)

    load_field(cot)

    def top(p, carry):
        grad = jnp.concatenate(
            [field[2 * p + s].reshape(64, 1, 8, 128) for s in range(2)], axis=1
        )
        make_delta(2, p, grad.reshape(8, 8, 16, 128))
        return carry

    lax.fori_loop(0, 2, top, 0)
    for layer in (2, 1):
        e = 5 - layer
        faces_out(e)
        send_faces(e)
        spread_all()
        inner(e)
        conv_inner(e, layer, False)
        correlate(layer)
        sum_0(layer)
        if layer == 1:
            sum_1(2)
        arrive(e)
        halo(e, e)
        conv_halo(e, layer, False)

        def backward(p, carry):
            make_delta(layer - 1, p, part[p].astype(BF16).astype(F32))
            return carry

        lax.fori_loop(0, 2, backward, 0)
    spread_all()
    correlate(0)
    sum_0(0)
    sum_1(1)
    sum_2(2)
    sum_1(0)
    sum_2(1)
    sum_2(0)
    for layer in (2, 1, 0):
        sum_3(layer)
    for layer in range(LAYERS):
        sum_end(layer)


def write_kernel(act, units, out, grads):
    out[...] = act[...]
    for layer in range(LAYERS):
        for unit, pair in enumerate(UNIT_KERNELS):
            value = units[layer, unit].astype(F32)
            grads[layer, pair[0]] = value[:, 0:64]
            if len(pair) > 1:
                grads[layer, pair[1]] = swap_halves(value)[:, 0:64]


def local(features, weights, cotangent, neighbours):
    rows, cols = lax.axis_size("tx"), lax.axis_size("ty")
    vmem = pl.BlockSpec(memory_space=pltpu.VMEM)
    act, units = pl.pallas_call(
        functools.partial(kernel, rows, cols, 1.0 / math.sqrt(4 * rows * cols * BLK**3)),
        out_shape=(
            jax.ShapeDtypeStruct((4, 64, 512), BF16),
            jax.ShapeDtypeStruct((LAYERS, UNITS, 64, 128), BF16),
        ),
        in_specs=[vmem, vmem, vmem, pl.BlockSpec(memory_space=pltpu.SMEM)],
        out_specs=(vmem, vmem),
        scratch_shapes=[
            pltpu.SMEM((4 * 27 * 3,), jnp.int32),
            pltpu.VMEM((5, 64, 8, 128), F32),
            pltpu.VMEM((5, 2, 10, 10, 16, 256), BF16),
            pltpu.VMEM((3, 2, 8, 8, 16, 128), F32),
            pltpu.VMEM((3, 256, 768), BF16),
            pltpu.VMEM((2, 768, 256), BF16),
            pltpu.VMEM((2, 256, 1280), BF16),
            pltpu.VMEM((3, 256, 256), F32),
            pltpu.VMEM((2, 8, 8, 16, 128), F32),
            pltpu.VMEM((4, 5, 8, 128), F32),
            pltpu.SemaphoreType.DMA((5, 8)),
            pltpu.SemaphoreType.DMA((5, 8)),
            pltpu.SemaphoreType.DMA((LAYERS, 3)),
            pltpu.SemaphoreType.DMA((LAYERS, 3)),
        ]
        + [pltpu.VMEM((2, 9, 32, 128), BF16)] * 10
        + [pltpu.VMEM((4, 16, 128), BF16)] * 5
        + [pltpu.VMEM((4, 16, 128), BF16)] * 5
        + [pltpu.VMEM((UNITS, 64, 128), BF16)] * LAYERS
        + [pltpu.VMEM((cols, 64, 128), BF16)] * LAYERS
        + [pltpu.VMEM((rows, 64, 128), BF16)] * LAYERS
        + [pltpu.VMEM((UNITS, 64, 128), BF16)] * LAYERS,
        compiler_params=pltpu.CompilerParams(
            collective_id=0, has_side_effects=True, vmem_limit_bytes=56 * 1024 * 1024
        ),
    )(features, weights, cotangent, neighbours)
    return pl.pallas_call(
        write_kernel,
        out_shape=(
            jax.ShapeDtypeStruct((4, 64, 512), BF16),
            jax.ShapeDtypeStruct((LAYERS, 27, 64, 64), F32),
        ),
        in_specs=[vmem, vmem],
        out_specs=(vmem, vmem),
        compiler_params=pltpu.CompilerParams(vmem_limit_bytes=16 * 1024 * 1024),
    )(act, units)


def solution(mesh):
    placed = (P(("tx", "ty"), None, None), P(), P(("tx", "ty"), None, None), P(("tx", "ty"), None))
    return jax.shard_map(
        local,
        mesh=mesh,
        in_specs=placed,
        out_specs=(P(("tx", "ty"), None, None), P()),
        check_vma=False,
    )
```

```python
import functools
import math

import jax
import jax.numpy as jnp
from jax import lax
from jax.experimental import pallas as pl
from jax.experimental.pallas import tpu as pltpu
from jax.sharding import PartitionSpec as P

BLK = 8
LAYERS = 3
F32 = jnp.float32
BF16 = jnp.bfloat16
MESH = pl.DeviceIdType.MESH
DIRS = [(-1, -1), (-1, 1), (1, -1), (1, 1), (0, -1), (0, 1), (-1, 0), (1, 0)]
UNIT_KERNELS = (
    [(9 * dx + 3 * dy, 9 * dx + 3 * dy + 1) for dy in range(3) for dx in range(3)]
    + [(9 * dx + 2, 9 * dx + 5) for dx in range(3)]
    + [(8, 17), (26,)]
)
UNITS = len(UNIT_KERNELS)


def lane_iota(shape):
    return lax.broadcasted_iota(jnp.int32, shape, len(shape) - 1)


def swap_halves(value):
    return pltpu.roll(value, 64, len(value.shape) - 1)


def pack_cols(face):
    low, high = face[0:4], face[4:8]
    packed = jnp.where(lane_iota(low.shape) < 64, low, swap_halves(high))
    return packed.reshape(32, 128).astype(BF16)


def unpack_cols(packed):
    wide = packed.astype(F32).reshape(4, 8, 128)
    return jnp.concatenate([wide, swap_halves(wide)], axis=0)


def triple(below, here, above):
    z = lax.broadcasted_iota(jnp.int32, here.shape, 1)
    lane = lane_iota(here.shape)
    down = pltpu.roll(jnp.where(z == 7, below, here), 1, 1)
    up = pltpu.roll(jnp.where(z == 0, above, here), 7, 1)
    first = jnp.where(lane < 64, down, swap_halves(here))
    second = jnp.where(lane < 64, up, 0.0)
    return jnp.concatenate([first, second], axis=2)


def sigmoid(value):
    return 0.5 + 0.5 * jnp.tanh(0.5 * value)


def kernel(
    rows, cols, scale, feat, w, cot, nbr, out, grads,
    idx, field, zp, pre, wf, wb, d3t, raw, part, corner,
    send_sem, recv_sem, sum_send, sum_recv, *pools,
):
    px, py, pd, sd = pools[0:5], pools[5:10], pools[10:15], pools[15:20]
    mine, from_cols, from_rows, full = (pools[20 + 3 * n:23 + 3 * n] for n in range(4))
    r, c = lax.axis_index("tx"), lax.axis_index("ty")

    def peer(dr, dc):
        return (lax.rem(r + dr + rows, rows), lax.rem(c + dc + cols, cols))

    def inside(dr, dc):
        return (r + dr >= 0) & (r + dr < rows) & (c + dc >= 0) & (c + dc < cols)

    barrier = pltpu.get_barrier_semaphore()
    greeted = rows - 1 + cols - 1
    for dr, dc in DIRS[:4]:
        greeted = greeted + inside(dr, dc).astype(jnp.int32)

        @pl.when(inside(dr, dc))
        def _():
            pl.semaphore_signal(barrier, inc=1, device_id=peer(dr, dc), device_id_type=MESH)

    for dr, dc in [(0, k) for k in range(1, cols)] + [(k, 0) for k in range(1, rows)]:
        pl.semaphore_signal(barrier, inc=1, device_id=peer(dr, dc), device_id_type=MESH)

    def fill_idx(b, carry):
        for o in range(27):
            ox, oy = o // 9 - 1, o // 3 % 3 - 1
            n = nbr[b, o]
            there = n >= 0
            n = jnp.maximum(n, 0)
            slot = n & 3
            dev = n >> 2
            same_r, same_c = (dev // cols) == r, (dev % cols) == c
            base = (b * 27 + o) * 3
            if ox == 0 and oy == 0:
                idx[base] = jnp.where(there, slot, 4)
            elif oy == 0:
                idx[base] = jnp.where(there, slot + jnp.where(same_r, 0, 4), 8)
            elif ox == 0:
                idx[base] = jnp.where(there, slot + jnp.where(same_c, 0, 4), 8)
            else:
                idx[base] = jnp.where(there & same_c, slot + jnp.where(same_r, 0, 4), 8)
                idx[base + 1] = jnp.where(
                    there & same_r & jnp.logical_not(same_c), slot + 4, 8
                )
                idx[base + 2] = jnp.where(
                    there & jnp.logical_not(same_r) & jnp.logical_not(same_c), slot, 4
                )
        return carry

    lax.fori_loop(0, 4, fill_idx, 0)

    field[4] = jnp.zeros((64, 8, 128), F32)
    for e in range(5):
        for s in range(2):
            px[e][s, 8] = jnp.zeros((32, 128), BF16)
            py[e][s, 8] = jnp.zeros((32, 128), BF16)
        for p in range(2):
            for y in (0, 9):
                zp[e, p, 1:9, y] = jnp.zeros((8, 16, 256), BF16)
    for q in range(4):
        corner[q, 4] = jnp.zeros((8, 128), F32)

    def load_field(source):
        def one(s, carry):
            wide = source[s].astype(F32)
            wide = jnp.concatenate([wide, jnp.zeros((64, 512), F32)], axis=0)
            field[s] = wide.T.reshape(64, 8, 128)
            return carry

        lax.fori_loop(0, 4, one, 0)

    def build_wf(layer):
        for dx in range(3):
            rows_here = []
            for dy in range(3):
                for dz in range(3):
                    rows_here.append(w[layer, 9 * dx + 3 * dy + dz])
                rows_here.append(jnp.zeros((64, 64), BF16))
            wf[layer, dx * 64:(dx + 1) * 64, :] = jnp.concatenate(rows_here, axis=1)
        wf[layer, 192:256, :] = jnp.zeros((64, 768), BF16)

    def build_wb(layer):
        for dy in range(3):
            for dz in range(3):
                row = dy * 256 + dz * 64
                parts = [w[layer, 26 - (9 * dx + 3 * dy + dz)] for dx in range(3)]
                parts.append(jnp.zeros((64, 64), BF16))
                wb[layer - 1, row:row + 64, :] = jnp.concatenate(parts, axis=1)
            wb[layer - 1, dy * 256 + 192:dy * 256 + 256, :] = jnp.zeros((64, 256), BF16)

    def copies(e):
        made = []
        for k, (dr, dc) in enumerate(DIRS):
            if dc == 0:
                s = 0 if dr > 0 else 1
                src, dst = px[e].at[s, pl.ds(0, 4)], px[e].at[s, pl.ds(4, 4)]
            elif dr == 0:
                s = 0 if dc > 0 else 1
                src, dst = py[e].at[s, pl.ds(0, 4)], py[e].at[s, pl.ds(4, 4)]
            else:
                q = (0 if dr > 0 else 1) * 2 + (0 if dc > 0 else 1)
                src, dst = sd[e].at[q], pd[e].at[q]
            copy = (
                pltpu.make_async_remote_copy(
                    src_ref=src, dst_ref=dst, send_sem=send_sem.at[e, k],
                    recv_sem=recv_sem.at[e, k], device_id=peer(dr, dc), device_id_type=MESH,
                )
            )
            made.append((inside(dr, dc), inside(-dr, -dc), copy))
        return made

    def arrive(e):
        for sends, receives, copy in copies(e):
            pl.when(sends)(copy.wait_send)
            pl.when(receives)(copy.wait_recv)

    def faces_out(e):
        def one(s, carry):
            for sx in range(2):
                x = 7 if sx == 0 else 0
                face = field[s, pl.ds(x * 8, 8)]
                px[e][sx, s] = pack_cols(face)
                for sy in range(2):
                    y = 7 if sy == 0 else 0
                    corner[sx * 2 + sy, s] = face[y]
            for sy in range(2):
                y = 7 if sy == 0 else 0
                face = jnp.concatenate([field[s, pl.ds(x * 8 + y, 1)] for x in range(8)], axis=0)
                py[e][sy, s] = pack_cols(face)
            return carry

        lax.fori_loop(0, 4, one, 0, unroll=2)
        lane = lane_iota((16, 128))
        for q in range(4):
            low = corner[q, 0:2].reshape(16, 128)
            high = corner[q, 2:4].reshape(16, 128)
            sd[e][q] = jnp.where(lane < 64, low, swap_halves(high)).astype(BF16)

    def send_faces(e):
        for sends, _, copy in copies(e):
            pl.when(sends)(copy.start)

    def at(b, o, which=0):
        return idx[(b * 27 + o) * 3 + which]

    def put(z, p, xs, ys, values):
        both = jnp.concatenate(values, axis=1).astype(BF16)
        zp[z, p, xs, ys] = both.reshape(zp[z, p, xs, ys].shape)

    def inner(z):
        def one(t, carry):
            p, x = t // 8, t % 8
            values = []
            for s in range(2):
                b = 2 * p + s
                take = [field[at(b, 12 + j), pl.ds(x * 8, 8)] for j in range(3)]
                values.append(triple(*take))
            put(z, p, pl.ds(x + 1, 1), pl.ds(1, 8), values)
            return carry

        lax.fori_loop(0, 16, one, 0, unroll=4)

    def halo(z, e):
        for q in range(4):
            wide = pd[e][q].astype(F32)
            corner[q, 0:2] = wide.reshape(2, 8, 128)
            corner[q, 2:4] = swap_halves(wide).reshape(2, 8, 128)

        def one(p, carry):
            for sx in range(2):
                ox, cell = 2 * sx - 1, 9 * sx
                values = []
                for s in range(2):
                    o = 9 * (ox + 1) + 3
                    take = [unpack_cols(px[e][sx, at(2 * p + s, o + j)]) for j in range(3)]
                    values.append(triple(*take))
                put(z, p, pl.ds(cell, 1), pl.ds(1, 8), values)
            for sy in range(2):
                oy, cell = 2 * sy - 1, 9 * sy
                values = []
                for s in range(2):
                    o = 9 + 3 * (oy + 1)
                    take = [unpack_cols(py[e][sy, at(2 * p + s, o + j)]) for j in range(3)]
                    values.append(triple(*take))
                put(z, p, pl.ds(1, 8), pl.ds(cell, 1), values)
            for sx in range(2):
                for sy in range(2):
                    values = []
                    for s in range(2):
                        take = []
                        for j in range(3):
                            o = 18 * sx + 6 * sy + j
                            b = 2 * p + s
                            ix, iy, iq = at(b, o), at(b, o, 1), at(b, o, 2)
                            if sy == 0:
                                from_x = swap_halves(px[e][sx, ix, 16:32].astype(F32)[8:16])
                            else:
                                from_x = px[e][sx, ix, 0:16].astype(F32)[0:8]
                            if sx == 0:
                                from_y = swap_halves(py[e][sy, iy, 16:32].astype(F32)[8:16])
                            else:
                                from_y = py[e][sy, iy, 0:16].astype(F32)[0:8]
                            total = from_x + from_y + corner[sx * 2 + sy, iq]
                            take.append(total.reshape(1, 8, 128))
                        values.append(triple(*take))
                    put(z, p, pl.ds(9 * sx, 1), pl.ds(9 * sy, 1), values)
            return carry

        lax.fori_loop(0, 2, one, 0, unroll=True)

    def multiply(stack, layer, forward, dy=None):
        at_dy = slice(0, 768) if dy is None else slice(dy * 256, dy * 256 + 256)
        if forward:
            return lax.dot_general(
                stack, wf[layer, :, at_dy], (((1,), (1,)), ((), ())), preferred_element_type=F32
            )
        return jnp.dot(stack, wb[layer - 1, at_dy, :], preferred_element_type=F32)

    def over_dx(acc):
        low, high = acc[..., 0:128], acc[..., 128:256]
        blank = jnp.zeros_like(low[0:1])
        left = jnp.concatenate([blank, low[0:7]], axis=0)
        right = jnp.concatenate([high[1:8], blank], axis=0)
        return left + swap_halves(low) + right

    def conv_inner(z, layer, forward):
        def one(p, carry):
            stack = jnp.concatenate(
                [zp[z, p, 1:9, dy:dy + 8].reshape(1024, 256) for dy in range(3)], axis=1
            )
            part[p] = over_dx(multiply(stack, layer, forward).reshape(8, 8, 16, 256))
            return carry

        lax.fori_loop(0, 2, one, 0)

    def conv_halo(z, layer, forward):
        planes = jnp.concatenate(
            [
                jnp.concatenate(
                    [zp[z, p, x, dy:dy + 8].reshape(128, 256) for dy in range(3)], axis=1
                )
                for x in (0, 9)
                for p in range(2)
            ],
            axis=0,
        )
        acc = multiply(planes, layer, forward).reshape(2, 2, 8, 16, 256)
        for p in range(2):
            part[p, 0] += acc[0, p, :, :, 0:128]
            part[p, 7] += acc[1, p, :, :, 128:256]
        for cell, dy, y in ((0, 0, 0), (9, 2, 7)):
            lines = jnp.concatenate(
                [zp[z, p, 1:9, cell].reshape(128, 256) for p in range(2)], axis=0
            )
            acc = multiply(lines, layer, forward, dy).reshape(2, 8, 16, 256)
            for p in range(2):
                part[p, :, y] += over_dx(acc[p])

    def to_field(p, value):
        value = value.reshape(64, 2, 8, 128)
        for s in range(2):
            field[2 * p + s] = value[:, s]

    def correlate(layer):
        for dy in range(3):
            total = jnp.zeros((192, 256), F32)
            for p in range(2):
                z = zp[layer, p, :, dy:dy + 8].reshape(1280, 256)
                total = total + jnp.dot(d3t[p], z, preferred_element_type=F32)
            raw[dy] = total
        lane = lane_iota((64, 128))
        for dx in range(3):
            at_dx = slice(dx * 64, dx * 64 + 64)
            for dy in range(3):
                mine[layer][dy * 3 + dx] = raw[dy, at_dx, 0:128].astype(BF16)
            pair = jnp.where(
                lane < 64, raw[0, at_dx, 128:256], swap_halves(raw[1, at_dx, 128:256])
            )
            mine[layer][9 + dx] = pair.astype(BF16)
        pair = jnp.where(lane < 64, raw[2, 0:64, 128:256], swap_halves(raw[2, 64:128, 128:256]))
        mine[layer][12] = pair.astype(BF16)
        mine[layer][13] = raw[2, 128:192, 128:256].astype(BF16)

    has_unit = c < UNITS

    def wait_bytes(ref, count, sem):
        part = ref.at[pl.ds(0, count)]
        pltpu.make_async_copy(part, part, sem).wait()

    def sum_copy(layer, phase, src, dst, device):
        return pltpu.make_async_remote_copy(
            src_ref=src, dst_ref=dst, send_sem=sum_send.at[layer, phase],
            recv_sem=sum_recv.at[layer, phase], device_id=device, device_id_type=MESH,
        )

    def over(size, body):
        def one(k, carry):
            body(k)
            return carry

        lax.fori_loop(1, size, one, 0)

    def sum_0(layer):
        def send(k):
            to = lax.rem(c + k, cols)

            @pl.when(to < UNITS)
            def _():
                sum_copy(layer, 0, mine[layer].at[to], from_cols[layer].at[c], (r, to)).start()

        over(cols, send)

    def sum_1(layer):
        @pl.when(has_unit)
        def _():
            wait_bytes(from_cols[layer], cols - 1, sum_recv.at[layer, 0])
            from_cols[layer][c] = mine[layer][c]
            total = from_cols[layer][0].astype(F32)
            for k in range(1, cols):
                total = total + from_cols[layer][k].astype(F32)
            from_rows[layer][r] = total.astype(BF16)

            def send(k):
                to = lax.rem(r + k, rows)
                sum_copy(
                    layer, 1, from_rows[layer].at[r], from_rows[layer].at[r], (to, c)
                ).start()

            over(rows, send)

    def sum_2(layer):
        @pl.when(has_unit)
        def _():
            wait_bytes(from_rows[layer], rows - 1, sum_recv.at[layer, 1])
            total = from_rows[layer][0].astype(F32)
            for k in range(1, rows):
                total = total + from_rows[layer][k].astype(F32)
            full[layer][c] = (total * scale).astype(BF16)

            def send(k):
                to = lax.rem(c + k, cols)
                sum_copy(layer, 2, full[layer].at[c], full[layer].at[c], (r, to)).start()

            over(cols, send)

    def sum_3(layer):
        @pl.when(has_unit)
        def _():
            wait_bytes(full[layer], UNITS - 1, sum_recv.at[layer, 2])

        @pl.when(jnp.logical_not(has_unit))
        def _():
            wait_bytes(full[layer], UNITS, sum_recv.at[layer, 2])

        grads[layer] = full[layer][...]

    def sum_end(layer):
        @pl.when(has_unit)
        def _():
            wait_bytes(mine[layer], UNITS - 1, sum_send.at[layer, 0])
            wait_bytes(from_rows[layer], rows - 1, sum_send.at[layer, 1])
            wait_bytes(from_cols[layer], cols - 1, sum_send.at[layer, 2])

        @pl.when(jnp.logical_not(has_unit))
        def _():
            wait_bytes(mine[layer], UNITS, sum_send.at[layer, 0])

    def spread(p, delta):
        lane = lane_iota((10, 8, 16, 128))
        zeros = jnp.zeros((2, 8, 16, 128), F32)
        wide = jnp.concatenate([zeros, delta, zeros], axis=0)
        first = jnp.where(lane < 64, wide[2:12], swap_halves(wide[1:11]))
        second = jnp.where(lane < 64, wide[0:10], 0.0)
        both = jnp.concatenate([first, second], axis=3).reshape(1280, 256)
        d3t[p] = both.T[0:192].astype(BF16)

    load_field(feat)
    faces_out(0)
    pl.semaphore_wait(barrier, greeted)
    send_faces(0)
    inner(0)
    build_wf(0)
    conv_inner(0, 0, True)
    for layer in (1, 2):
        build_wf(layer)
        build_wb(layer)

    for layer in range(LAYERS):
        if layer > 0:
            faces_out(layer)
            send_faces(layer)
            inner(layer)
            conv_inner(layer, layer, True)
        arrive(layer)
        halo(layer, layer)
        conv_halo(layer, layer, True)

        def forward(p, carry):
            value = part[p]
            pre[layer, p] = value
            act = (value * sigmoid(value)).astype(BF16).astype(F32)
            to_field(p, act)
            return carry

        lax.fori_loop(0, 2, forward, 0)

    def store_out(s, carry):
        out[s] = field[s].reshape(512, 128).T[0:64].astype(BF16)
        return carry

    lax.fori_loop(0, 4, store_out, 0)

    def make_delta(layer, p, grad):
        v = pre[layer, p]
        s = sigmoid(v)
        delta = (grad * (s * (1.0 + v * (1.0 - s)))).astype(BF16).astype(F32)
        part[p] = delta
        to_field(p, delta)

    def spread_all():
        def one(p, carry):
            spread(p, part[p])
            return carry

        lax.fori_loop(0, 2, one, 0)

    load_field(cot)

    def top(p, carry):
        grad = jnp.concatenate(
            [field[2 * p + s].reshape(64, 1, 8, 128) for s in range(2)], axis=1
        )
        make_delta(2, p, grad.reshape(8, 8, 16, 128))
        return carry

    lax.fori_loop(0, 2, top, 0)
    for layer in (2, 1):
        e = 5 - layer
        faces_out(e)
        send_faces(e)
        spread_all()
        inner(e)
        conv_inner(e, layer, False)
        correlate(layer)
        sum_0(layer)
        if layer == 1:
            sum_1(2)
        arrive(e)
        halo(e, e)
        conv_halo(e, layer, False)

        def backward(p, carry):
            make_delta(layer - 1, p, part[p].astype(BF16).astype(F32))
            return carry

        lax.fori_loop(0, 2, backward, 0)
    spread_all()
    correlate(0)
    sum_0(0)
    sum_1(1)
    sum_2(2)
    sum_1(0)
    sum_2(1)
    sum_2(0)
    for layer in (2, 1, 0):
        sum_3(layer)
    for layer in range(LAYERS):
        sum_end(layer)


def write_kernel(act, units, out, grads, held, sems):
    copies = [pltpu.make_async_copy(act, out, sems.at[LAYERS])] + [
        pltpu.make_async_copy(units.at[layer], held.at[layer], sems.at[layer])
        for layer in range(LAYERS)
    ]
    for copy in copies:
        copy.start()
    for layer in range(LAYERS):
        copies[layer + 1].wait()
        for unit, pair in enumerate(UNIT_KERNELS):
            value = held[layer, unit].astype(F32)
            grads[layer, pair[0]] = value[:, 0:64]
            if len(pair) > 1:
                grads[layer, pair[1]] = swap_halves(value)[:, 0:64]
    copies[0].wait()


def local(features, weights, cotangent, neighbours):
    rows, cols = lax.axis_size("tx"), lax.axis_size("ty")
    vmem = pl.BlockSpec(memory_space=pltpu.VMEM)
    hbm = pl.BlockSpec(memory_space=pltpu.HBM)
    act, units = pl.pallas_call(
        functools.partial(kernel, rows, cols, 1.0 / math.sqrt(4 * rows * cols * BLK**3)),
        out_shape=(
            jax.ShapeDtypeStruct((4, 64, 512), BF16),
            jax.ShapeDtypeStruct((LAYERS, UNITS, 64, 128), BF16),
        ),
        in_specs=[vmem, vmem, vmem, pl.BlockSpec(memory_space=pltpu.SMEM)],
        out_specs=(vmem, vmem),
        scratch_shapes=[
            pltpu.SMEM((4 * 27 * 3,), jnp.int32),
            pltpu.VMEM((5, 64, 8, 128), F32),
            pltpu.VMEM((5, 2, 10, 10, 16, 256), BF16),
            pltpu.VMEM((3, 2, 8, 8, 16, 128), F32),
            pltpu.VMEM((3, 256, 768), BF16),
            pltpu.VMEM((2, 768, 256), BF16),
            pltpu.VMEM((2, 192, 1280), BF16),
            pltpu.VMEM((3, 192, 256), F32),
            pltpu.VMEM((2, 8, 8, 16, 128), F32),
            pltpu.VMEM((4, 5, 8, 128), F32),
            pltpu.SemaphoreType.DMA((5, 8)),
            pltpu.SemaphoreType.DMA((5, 8)),
            pltpu.SemaphoreType.DMA((LAYERS, 3)),
            pltpu.SemaphoreType.DMA((LAYERS, 3)),
        ]
        + [pltpu.VMEM((2, 9, 32, 128), BF16)] * 10
        + [pltpu.VMEM((4, 16, 128), BF16)] * 5
        + [pltpu.VMEM((4, 16, 128), BF16)] * 5
        + [pltpu.VMEM((UNITS, 64, 128), BF16)] * LAYERS
        + [pltpu.VMEM((cols, 64, 128), BF16)] * LAYERS
        + [pltpu.VMEM((rows, 64, 128), BF16)] * LAYERS
        + [pltpu.VMEM((UNITS, 64, 128), BF16)] * LAYERS,
        compiler_params=pltpu.CompilerParams(
            collective_id=0, has_side_effects=True, vmem_limit_bytes=56 * 1024 * 1024
        ),
    )(features, weights, cotangent, neighbours)
    return pl.pallas_call(
        write_kernel,
        out_shape=(
            jax.ShapeDtypeStruct((4, 64, 512), BF16),
            jax.ShapeDtypeStruct((LAYERS, 27, 64, 64), F32),
        ),
        in_specs=[hbm, hbm],
        out_specs=(hbm, vmem),
        scratch_shapes=[
            pltpu.VMEM((LAYERS, UNITS, 64, 128), BF16),
            pltpu.SemaphoreType.DMA((LAYERS + 1,)),
        ],
        compiler_params=pltpu.CompilerParams(vmem_limit_bytes=56 * 1024 * 1024),
    )(act, units)


def solution(mesh):
    placed = (P(("tx", "ty"), None, None), P(), P(("tx", "ty"), None, None), P(("tx", "ty"), None))
    return jax.shard_map(
        local,
        mesh=mesh,
        in_specs=placed,
        out_specs=(P(("tx", "ty"), None, None), P()),
        check_vma=False,
    )
```

```python
import functools
import math

import jax
import jax.numpy as jnp
from jax import lax
from jax.experimental import pallas as pl
from jax.experimental.pallas import tpu as pltpu
from jax.sharding import PartitionSpec as P

BLK = 8
LAYERS = 3
F32 = jnp.float32
BF16 = jnp.bfloat16
MESH = pl.DeviceIdType.MESH
DIRS = [(-1, -1), (-1, 1), (1, -1), (1, 1), (0, -1), (0, 1), (-1, 0), (1, 0)]
UNIT_KERNELS = (
    [(9 * dx + 3 * dy, 9 * dx + 3 * dy + 1) for dy in range(3) for dx in range(3)]
    + [(9 * dx + 2, 9 * dx + 5) for dx in range(3)]
    + [(8, 17), (26,)]
)
UNITS = len(UNIT_KERNELS)


def lane_iota(shape):
    return lax.broadcasted_iota(jnp.int32, shape, len(shape) - 1)


def swap_halves(value):
    return pltpu.roll(value, 64, len(value.shape) - 1)


def pack_cols(face):
    low, high = face[0:4], face[4:8]
    packed = jnp.where(lane_iota(low.shape) < 64, low, swap_halves(high))
    return packed.reshape(32, 128).astype(BF16)


def unpack_cols(packed):
    wide = packed.astype(F32).reshape(4, 8, 128)
    return jnp.concatenate([wide, swap_halves(wide)], axis=0)


def triple(below, here, above):
    z = lax.broadcasted_iota(jnp.int32, here.shape, 1)
    lane = lane_iota(here.shape)
    down = pltpu.roll(jnp.where(z == 7, below, here), 1, 1)
    up = pltpu.roll(jnp.where(z == 0, above, here), 7, 1)
    first = jnp.where(lane < 64, down, swap_halves(here))
    second = jnp.where(lane < 64, up, 0.0)
    return jnp.concatenate([first, second], axis=2)


def sigmoid(value):
    return 0.5 + 0.5 * jnp.tanh(0.5 * value)


def kernel(
    rows, cols, scale, feat, w, cot, nbr, out, grads,
    idx, field, zp, pre, wf, wb, d3t, raw, part, corner,
    send_sem, recv_sem, sum_send, sum_recv, *pools,
):
    px, py, pd, sd = pools[0:5], pools[5:10], pools[10:15], pools[15:20]
    mine, from_cols, from_rows, full = (pools[20 + 3 * n:23 + 3 * n] for n in range(4))
    r, c = lax.axis_index("tx"), lax.axis_index("ty")

    def peer(dr, dc):
        return (lax.rem(r + dr + rows, rows), lax.rem(c + dc + cols, cols))

    def inside(dr, dc):
        return (r + dr >= 0) & (r + dr < rows) & (c + dc >= 0) & (c + dc < cols)

    barrier = pltpu.get_barrier_semaphore()
    greeted = rows - 1 + cols - 1
    for dr, dc in DIRS[:4]:
        greeted = greeted + inside(dr, dc).astype(jnp.int32)

        @pl.when(inside(dr, dc))
        def _():
            pl.semaphore_signal(barrier, inc=1, device_id=peer(dr, dc), device_id_type=MESH)

    for dr, dc in [(0, k) for k in range(1, cols)] + [(k, 0) for k in range(1, rows)]:
        pl.semaphore_signal(barrier, inc=1, device_id=peer(dr, dc), device_id_type=MESH)

    def fill_idx(b, carry):
        for o in range(27):
            ox, oy = o // 9 - 1, o // 3 % 3 - 1
            n = nbr[b, o]
            there = n >= 0
            n = jnp.maximum(n, 0)
            slot = n & 3
            dev = n >> 2
            same_r, same_c = (dev // cols) == r, (dev % cols) == c
            base = (b * 27 + o) * 3
            if ox == 0 and oy == 0:
                idx[base] = jnp.where(there, slot, 4)
            elif oy == 0:
                idx[base] = jnp.where(there, slot + jnp.where(same_r, 0, 4), 8)
            elif ox == 0:
                idx[base] = jnp.where(there, slot + jnp.where(same_c, 0, 4), 8)
            else:
                idx[base] = jnp.where(there & same_c, slot + jnp.where(same_r, 0, 4), 8)
                idx[base + 1] = jnp.where(
                    there & same_r & jnp.logical_not(same_c), slot + 4, 8
                )
                idx[base + 2] = jnp.where(
                    there & jnp.logical_not(same_r) & jnp.logical_not(same_c), slot, 4
                )
        return carry

    lax.fori_loop(0, 4, fill_idx, 0)

    field[4] = jnp.zeros((64, 8, 128), F32)
    for e in range(5):
        for s in range(2):
            px[e][s, 8] = jnp.zeros((32, 128), BF16)
            py[e][s, 8] = jnp.zeros((32, 128), BF16)
        for p in range(2):
            for y in (0, 9):
                zp[e, p, 1:9, y] = jnp.zeros((8, 16, 256), BF16)
    for q in range(4):
        corner[q, 4] = jnp.zeros((8, 128), F32)

    def load_field(source):
        def one(s, carry):
            wide = source[s].astype(F32)
            wide = jnp.concatenate([wide, jnp.zeros((64, 512), F32)], axis=0)
            field[s] = wide.T.reshape(64, 8, 128)
            return carry

        lax.fori_loop(0, 4, one, 0)

    def build_wf(layer):
        for dx in range(3):
            rows_here = []
            for dy in range(3):
                for dz in range(3):
                    rows_here.append(w[layer, 9 * dx + 3 * dy + dz])
                rows_here.append(jnp.zeros((64, 64), BF16))
            wf[layer, dx * 64:(dx + 1) * 64, :] = jnp.concatenate(rows_here, axis=1)
        wf[layer, 192:256, :] = jnp.zeros((64, 768), BF16)

    def build_wb(layer):
        for dy in range(3):
            for dz in range(3):
                row = dy * 256 + dz * 64
                parts = [w[layer, 26 - (9 * dx + 3 * dy + dz)] for dx in range(3)]
                parts.append(jnp.zeros((64, 64), BF16))
                wb[layer - 1, row:row + 64, :] = jnp.concatenate(parts, axis=1)
            wb[layer - 1, dy * 256 + 192:dy * 256 + 256, :] = jnp.zeros((64, 256), BF16)

    def copies(e):
        made = []
        for k, (dr, dc) in enumerate(DIRS):
            if dc == 0:
                s = 0 if dr > 0 else 1
                src, dst = px[e].at[s, pl.ds(0, 4)], px[e].at[s, pl.ds(4, 4)]
            elif dr == 0:
                s = 0 if dc > 0 else 1
                src, dst = py[e].at[s, pl.ds(0, 4)], py[e].at[s, pl.ds(4, 4)]
            else:
                q = (0 if dr > 0 else 1) * 2 + (0 if dc > 0 else 1)
                src, dst = sd[e].at[q], pd[e].at[q]
            copy = (
                pltpu.make_async_remote_copy(
                    src_ref=src, dst_ref=dst, send_sem=send_sem.at[e, k],
                    recv_sem=recv_sem.at[e, k], device_id=peer(dr, dc), device_id_type=MESH,
                )
            )
            made.append((inside(dr, dc), inside(-dr, -dc), copy))
        return made

    def arrive(e):
        for sends, receives, copy in copies(e):
            pl.when(sends)(copy.wait_send)
            pl.when(receives)(copy.wait_recv)

    def faces_out(e):
        def one(s, carry):
            for sx in range(2):
                x = 7 if sx == 0 else 0
                face = field[s, pl.ds(x * 8, 8)]
                px[e][sx, s] = pack_cols(face)
                for sy in range(2):
                    y = 7 if sy == 0 else 0
                    corner[sx * 2 + sy, s] = face[y]
            for sy in range(2):
                y = 7 if sy == 0 else 0
                face = jnp.concatenate([field[s, pl.ds(x * 8 + y, 1)] for x in range(8)], axis=0)
                py[e][sy, s] = pack_cols(face)
            return carry

        lax.fori_loop(0, 4, one, 0, unroll=2)
        lane = lane_iota((16, 128))
        for q in range(4):
            low = corner[q, 0:2].reshape(16, 128)
            high = corner[q, 2:4].reshape(16, 128)
            sd[e][q] = jnp.where(lane < 64, low, swap_halves(high)).astype(BF16)

    def send_faces(e):
        for sends, _, copy in copies(e):
            pl.when(sends)(copy.start)

    def at(b, o, which=0):
        return idx[(b * 27 + o) * 3 + which]

    def put(z, p, xs, ys, values):
        both = jnp.concatenate(values, axis=1).astype(BF16)
        zp[z, p, xs, ys] = both.reshape(zp[z, p, xs, ys].shape)

    def inner(z):
        def one(t, carry):
            p, x = t // 8, t % 8
            values = []
            for s in range(2):
                b = 2 * p + s
                take = [field[at(b, 12 + j), pl.ds(x * 8, 8)] for j in range(3)]
                values.append(triple(*take))
            put(z, p, pl.ds(x + 1, 1), pl.ds(1, 8), values)
            return carry

        lax.fori_loop(0, 16, one, 0, unroll=4)

    def halo(z, e):
        for q in range(4):
            wide = pd[e][q].astype(F32)
            corner[q, 0:2] = wide.reshape(2, 8, 128)
            corner[q, 2:4] = swap_halves(wide).reshape(2, 8, 128)

        def one(p, carry):
            for sx in range(2):
                ox, cell = 2 * sx - 1, 9 * sx
                values = []
                for s in range(2):
                    o = 9 * (ox + 1) + 3
                    take = [unpack_cols(px[e][sx, at(2 * p + s, o + j)]) for j in range(3)]
                    values.append(triple(*take))
                put(z, p, pl.ds(cell, 1), pl.ds(1, 8), values)
            for sy in range(2):
                oy, cell = 2 * sy - 1, 9 * sy
                values = []
                for s in range(2):
                    o = 9 + 3 * (oy + 1)
                    take = [unpack_cols(py[e][sy, at(2 * p + s, o + j)]) for j in range(3)]
                    values.append(triple(*take))
                put(z, p, pl.ds(1, 8), pl.ds(cell, 1), values)
            for sx in range(2):
                for sy in range(2):
                    values = []
                    for s in range(2):
                        take = []
                        for j in range(3):
                            o = 18 * sx + 6 * sy + j
                            b = 2 * p + s
                            ix, iy, iq = at(b, o), at(b, o, 1), at(b, o, 2)
                            if sy == 0:
                                from_x = swap_halves(px[e][sx, ix, 16:32].astype(F32)[8:16])
                            else:
                                from_x = px[e][sx, ix, 0:16].astype(F32)[0:8]
                            if sx == 0:
                                from_y = swap_halves(py[e][sy, iy, 16:32].astype(F32)[8:16])
                            else:
                                from_y = py[e][sy, iy, 0:16].astype(F32)[0:8]
                            total = from_x + from_y + corner[sx * 2 + sy, iq]
                            take.append(total.reshape(1, 8, 128))
                        values.append(triple(*take))
                    put(z, p, pl.ds(9 * sx, 1), pl.ds(9 * sy, 1), values)
            return carry

        lax.fori_loop(0, 2, one, 0, unroll=True)

    def multiply(stack, layer, forward, dy=None):
        at_dy = slice(0, 768) if dy is None else slice(dy * 256, dy * 256 + 256)
        if forward:
            return lax.dot_general(
                stack, wf[layer, :, at_dy], (((1,), (1,)), ((), ())), preferred_element_type=F32
            )
        return jnp.dot(stack, wb[layer - 1, at_dy, :], preferred_element_type=F32)

    def over_dx(acc):
        low, high = acc[..., 0:128], acc[..., 128:256]
        blank = jnp.zeros_like(low[0:1])
        left = jnp.concatenate([blank, low[0:7]], axis=0)
        right = jnp.concatenate([high[1:8], blank], axis=0)
        return left + swap_halves(low) + right

    def conv_inner(z, layer, forward):
        def one(p, carry):
            stack = jnp.concatenate(
                [zp[z, p, 1:9, dy:dy + 8].reshape(1024, 256) for dy in range(3)], axis=1
            )
            part[p] = over_dx(multiply(stack, layer, forward).reshape(8, 8, 16, 256))
            return carry

        lax.fori_loop(0, 2, one, 0)

    def conv_halo(z, layer, forward):
        planes = jnp.concatenate(
            [
                jnp.concatenate(
                    [zp[z, p, x, dy:dy + 8].reshape(128, 256) for dy in range(3)], axis=1
                )
                for x in (0, 9)
                for p in range(2)
            ],
            axis=0,
        )
        acc = multiply(planes, layer, forward).reshape(2, 2, 8, 16, 256)
        for p in range(2):
            part[p, 0] += acc[0, p, :, :, 0:128]
            part[p, 7] += acc[1, p, :, :, 128:256]
        for cell, dy, y in ((0, 0, 0), (9, 2, 7)):
            lines = jnp.concatenate(
                [zp[z, p, 1:9, cell].reshape(128, 256) for p in range(2)], axis=0
            )
            acc = multiply(lines, layer, forward, dy).reshape(2, 8, 16, 256)
            for p in range(2):
                part[p, :, y] += over_dx(acc[p])

    def to_field(p, value):
        value = value.reshape(64, 2, 8, 128)
        for s in range(2):
            field[2 * p + s] = value[:, s]

    def correlate(layer):
        for dy in range(3):
            total = jnp.zeros((192, 256), F32)
            for p in range(2):
                z = zp[layer, p, :, dy:dy + 8].reshape(1280, 256)
                total = total + jnp.dot(d3t[p], z, preferred_element_type=F32)
            raw[dy] = total
        lane = lane_iota((64, 128))
        for dx in range(3):
            at_dx = slice(dx * 64, dx * 64 + 64)
            for dy in range(3):
                mine[layer][dy * 3 + dx] = raw[dy, at_dx, 0:128].astype(BF16)
            pair = jnp.where(
                lane < 64, raw[0, at_dx, 128:256], swap_halves(raw[1, at_dx, 128:256])
            )
            mine[layer][9 + dx] = pair.astype(BF16)
        pair = jnp.where(lane < 64, raw[2, 0:64, 128:256], swap_halves(raw[2, 64:128, 128:256]))
        mine[layer][12] = pair.astype(BF16)
        mine[layer][13] = raw[2, 128:192, 128:256].astype(BF16)

    has_unit = c < UNITS

    def wait_bytes(ref, count, sem):
        part = ref.at[pl.ds(0, count)]
        pltpu.make_async_copy(part, part, sem).wait()

    def sum_copy(layer, phase, src, dst, device):
        return pltpu.make_async_remote_copy(
            src_ref=src, dst_ref=dst, send_sem=sum_send.at[layer, phase],
            recv_sem=sum_recv.at[layer, phase], device_id=device, device_id_type=MESH,
        )

    def over(size, body):
        def one(k, carry):
            body(k)
            return carry

        lax.fori_loop(1, size, one, 0)

    def sum_0(layer):
        def send(k):
            to = lax.rem(c + k, cols)

            @pl.when(to < UNITS)
            def _():
                sum_copy(layer, 0, mine[layer].at[to], from_cols[layer].at[c], (r, to)).start()

        over(cols, send)

    def sum_1(layer):
        @pl.when(has_unit)
        def _():
            wait_bytes(from_cols[layer], cols - 1, sum_recv.at[layer, 0])
            from_cols[layer][c] = mine[layer][c]
            total = from_cols[layer][0].astype(F32)
            for k in range(1, cols):
                total = total + from_cols[layer][k].astype(F32)
            from_rows[layer][r] = total.astype(BF16)

            def send(k):
                to = lax.rem(r + k, rows)
                sum_copy(
                    layer, 1, from_rows[layer].at[r], from_rows[layer].at[r], (to, c)
                ).start()

            over(rows, send)

    def sum_2(layer):
        @pl.when(has_unit)
        def _():
            wait_bytes(from_rows[layer], rows - 1, sum_recv.at[layer, 1])
            total = from_rows[layer][0].astype(F32)
            for k in range(1, rows):
                total = total + from_rows[layer][k].astype(F32)
            full[layer][c] = (total * scale).astype(BF16)

            def send(k):
                to = lax.rem(c + k, cols)
                sum_copy(layer, 2, full[layer].at[c], full[layer].at[c], (r, to)).start()

            over(cols, send)

    def sum_3(layer):
        @pl.when(has_unit)
        def _():
            wait_bytes(full[layer], UNITS - 1, sum_recv.at[layer, 2])

        @pl.when(jnp.logical_not(has_unit))
        def _():
            wait_bytes(full[layer], UNITS, sum_recv.at[layer, 2])

        grads[layer] = full[layer][...]

    def sum_end(layer):
        @pl.when(has_unit)
        def _():
            wait_bytes(mine[layer], UNITS - 1, sum_send.at[layer, 0])
            wait_bytes(from_rows[layer], rows - 1, sum_send.at[layer, 1])
            wait_bytes(from_cols[layer], cols - 1, sum_send.at[layer, 2])

        @pl.when(jnp.logical_not(has_unit))
        def _():
            wait_bytes(mine[layer], UNITS, sum_send.at[layer, 0])

    def spread(p, delta):
        lane = lane_iota((10, 8, 16, 128))
        zeros = jnp.zeros((2, 8, 16, 128), F32)
        wide = jnp.concatenate([zeros, delta, zeros], axis=0)
        first = jnp.where(lane < 64, wide[2:12], swap_halves(wide[1:11]))
        second = jnp.where(lane < 64, wide[0:10], 0.0)
        both = jnp.concatenate([first, second], axis=3).reshape(1280, 256)
        d3t[p] = both.T[0:192].astype(BF16)

    load_field(feat)
    faces_out(0)
    pl.semaphore_wait(barrier, greeted)
    send_faces(0)
    inner(0)
    build_wf(0)
    conv_inner(0, 0, True)
    for layer in (1, 2):
        build_wf(layer)
        build_wb(layer)

    for layer in range(LAYERS):
        if layer > 0:
            faces_out(layer)
            send_faces(layer)
            inner(layer)
            conv_inner(layer, layer, True)
        arrive(layer)
        halo(layer, layer)
        conv_halo(layer, layer, True)

        def forward(p, carry):
            value = part[p]
            pre[layer, p] = value
            act = (value * sigmoid(value)).astype(BF16).astype(F32)
            to_field(p, act)
            return carry

        lax.fori_loop(0, 2, forward, 0)

    def store_out(s, carry):
        out[s] = field[s].reshape(512, 128).T[0:64].astype(BF16)
        return carry

    lax.fori_loop(0, 4, store_out, 0)

    def make_delta(layer, p, grad):
        v = pre[layer, p]
        s = sigmoid(v)
        delta = (grad * (s * (1.0 + v * (1.0 - s)))).astype(BF16).astype(F32)
        part[p] = delta
        to_field(p, delta)

    def spread_all():
        def one(p, carry):
            spread(p, part[p])
            return carry

        lax.fori_loop(0, 2, one, 0)

    load_field(cot)

    def top(p, carry):
        grad = jnp.concatenate(
            [field[2 * p + s].reshape(64, 1, 8, 128) for s in range(2)], axis=1
        )
        make_delta(2, p, grad.reshape(8, 8, 16, 128))
        return carry

    lax.fori_loop(0, 2, top, 0)
    for layer in (2, 1):
        e = 5 - layer
        faces_out(e)
        send_faces(e)
        spread_all()
        inner(e)
        conv_inner(e, layer, False)
        correlate(layer)
        sum_0(layer)
        if layer == 1:
            sum_1(2)
        arrive(e)
        halo(e, e)
        conv_halo(e, layer, False)

        def backward(p, carry):
            make_delta(layer - 1, p, part[p].astype(BF16).astype(F32))
            return carry

        lax.fori_loop(0, 2, backward, 0)
    spread_all()
    correlate(0)
    sum_0(0)
    sum_1(1)
    sum_2(2)
    sum_1(0)
    sum_2(1)
    sum_2(0)
    for layer in (2, 1, 0):
        sum_3(layer)
    for layer in range(LAYERS):
        sum_end(layer)


def write_kernel(act, units, out, grads):
    out[...] = act[...]
    for layer in range(LAYERS):
        for unit, pair in enumerate(UNIT_KERNELS):
            value = units[layer, unit].astype(F32)
            grads[layer, pair[0]] = value[:, 0:64]
            if len(pair) > 1:
                grads[layer, pair[1]] = swap_halves(value)[:, 0:64]


def local(features, weights, cotangent, neighbours):
    rows, cols = lax.axis_size("tx"), lax.axis_size("ty")
    vmem = pl.BlockSpec(memory_space=pltpu.VMEM)
    act, units = pl.pallas_call(
        functools.partial(kernel, rows, cols, 1.0 / math.sqrt(4 * rows * cols * BLK**3)),
        out_shape=(
            jax.ShapeDtypeStruct((4, 64, 512), BF16),
            jax.ShapeDtypeStruct((LAYERS, UNITS, 64, 128), BF16),
        ),
        in_specs=[vmem, vmem, vmem, pl.BlockSpec(memory_space=pltpu.SMEM)],
        out_specs=(vmem, vmem),
        scratch_shapes=[
            pltpu.SMEM((4 * 27 * 3,), jnp.int32),
            pltpu.VMEM((5, 64, 8, 128), F32),
            pltpu.VMEM((5, 2, 10, 10, 16, 256), BF16),
            pltpu.VMEM((3, 2, 8, 8, 16, 128), F32),
            pltpu.VMEM((3, 256, 768), BF16),
            pltpu.VMEM((2, 768, 256), BF16),
            pltpu.VMEM((2, 192, 1280), BF16),
            pltpu.VMEM((3, 192, 256), F32),
            pltpu.VMEM((2, 8, 8, 16, 128), F32),
            pltpu.VMEM((4, 5, 8, 128), F32),
            pltpu.SemaphoreType.DMA((5, 8)),
            pltpu.SemaphoreType.DMA((5, 8)),
            pltpu.SemaphoreType.DMA((LAYERS, 3)),
            pltpu.SemaphoreType.DMA((LAYERS, 3)),
        ]
        + [pltpu.VMEM((2, 9, 32, 128), BF16)] * 10
        + [pltpu.VMEM((4, 16, 128), BF16)] * 5
        + [pltpu.VMEM((4, 16, 128), BF16)] * 5
        + [pltpu.VMEM((UNITS, 64, 128), BF16)] * LAYERS
        + [pltpu.VMEM((cols, 64, 128), BF16)] * LAYERS
        + [pltpu.VMEM((rows, 64, 128), BF16)] * LAYERS
        + [pltpu.VMEM((UNITS, 64, 128), BF16)] * LAYERS,
        compiler_params=pltpu.CompilerParams(
            collective_id=0, has_side_effects=True, vmem_limit_bytes=56 * 1024 * 1024
        ),
    )(features, weights, cotangent, neighbours)
    return pl.pallas_call(
        write_kernel,
        out_shape=(
            jax.ShapeDtypeStruct((4, 64, 512), BF16),
            jax.ShapeDtypeStruct((LAYERS, 27, 64, 64), F32),
        ),
        in_specs=[vmem, vmem],
        out_specs=(vmem, vmem),
        compiler_params=pltpu.CompilerParams(vmem_limit_bytes=56 * 1024 * 1024),
    )(act, units)


def solution(mesh):
    placed = (P(("tx", "ty"), None, None), P(), P(("tx", "ty"), None, None), P(("tx", "ty"), None))
    return jax.shard_map(
        local,
        mesh=mesh,
        in_specs=placed,
        out_specs=(P(("tx", "ty"), None, None), P()),
        check_vma=False,
    )
```

```python
import functools
import math

import jax
import jax.numpy as jnp
from jax import lax
from jax.experimental import pallas as pl
from jax.experimental.pallas import tpu as pltpu
from jax.sharding import PartitionSpec as P

BLK = 8
LAYERS = 3
F32 = jnp.float32
BF16 = jnp.bfloat16
MESH = pl.DeviceIdType.MESH
DIRS = [(-1, -1), (-1, 1), (1, -1), (1, 1), (0, -1), (0, 1), (-1, 0), (1, 0)]
UNIT_KERNELS = (
    [(9 * dx + 3 * dy, 9 * dx + 3 * dy + 1) for dy in range(3) for dx in range(3)]
    + [(9 * dx + 2, 9 * dx + 5) for dx in range(3)]
    + [(8, 17), (26,)]
)
UNITS = len(UNIT_KERNELS)


def lane_iota(shape):
    return lax.broadcasted_iota(jnp.int32, shape, len(shape) - 1)


def swap_halves(value):
    return pltpu.roll(value, 64, len(value.shape) - 1)


def pack_cols(face):
    low, high = face[0:4], face[4:8]
    packed = jnp.where(lane_iota(low.shape) < 64, low, swap_halves(high))
    return packed.reshape(32, 128).astype(BF16)


def unpack_cols(packed):
    wide = packed.astype(F32).reshape(4, 8, 128)
    return jnp.concatenate([wide, swap_halves(wide)], axis=0)


def triple(below, here, above):
    z = lax.broadcasted_iota(jnp.int32, here.shape, 1)
    lane = lane_iota(here.shape)
    down = pltpu.roll(jnp.where(z == 7, below, here), 1, 1)
    up = pltpu.roll(jnp.where(z == 0, above, here), 7, 1)
    first = jnp.where(lane < 64, down, swap_halves(here))
    second = jnp.where(lane < 64, up, 0.0)
    return jnp.concatenate([first, second], axis=2)


def sigmoid(value):
    return 0.5 + 0.5 * jnp.tanh(0.5 * value)


def kernel(
    rows, cols, scale, feat, w_hbm, cot_hbm, nbr, out, grads,
    idx, field, zp, pre, wf, wb, d3t, raw, part, corner, last, top, w, cot, fetch_sem,
    send_sem, recv_sem, sum_send, sum_recv, *pools,
):
    px, py, pd, sd = pools[0:5], pools[5:10], pools[10:15], pools[15:20]
    mine, from_cols, from_rows, full = (pools[20 + 3 * n:23 + 3 * n] for n in range(4))
    r, c = lax.axis_index("tx"), lax.axis_index("ty")

    def peer(dr, dc):
        return (lax.rem(r + dr + rows, rows), lax.rem(c + dc + cols, cols))

    def inside(dr, dc):
        return (r + dr >= 0) & (r + dr < rows) & (c + dc >= 0) & (c + dc < cols)

    barrier = pltpu.get_barrier_semaphore()
    greeted = rows - 1 + cols - 1
    for dr, dc in DIRS[:4]:
        greeted = greeted + inside(dr, dc).astype(jnp.int32)

        @pl.when(inside(dr, dc))
        def _():
            pl.semaphore_signal(barrier, inc=1, device_id=peer(dr, dc), device_id_type=MESH)

    for dr, dc in [(0, k) for k in range(1, cols)] + [(k, 0) for k in range(1, rows)]:
        pl.semaphore_signal(barrier, inc=1, device_id=peer(dr, dc), device_id_type=MESH)

    fetch_w = pltpu.make_async_copy(w_hbm, w, fetch_sem.at[0])
    fetch_cot = pltpu.make_async_copy(cot_hbm, cot, fetch_sem.at[1])
    fetch_w.start()
    fetch_cot.start()

    def in_rows(block):
        wide = block.astype(F32)
        wide = jnp.concatenate([wide, jnp.zeros((64, 512), F32)], axis=0)
        return wide.T.reshape(64, 8, 128)

    def load_field():
        def one(s, carry):
            field[s] = in_rows(feat[s])
            return carry

        lax.fori_loop(0, 4, one, 0)

    def load_top():
        def one(p, carry):
            for s in range(2):
                top[p, :, s] = in_rows(cot[2 * p + s])
            return carry

        lax.fori_loop(0, 2, one, 0)

    def build_wf(layer):
        for dx in range(3):
            rows_here = []
            for dy in range(3):
                for dz in range(3):
                    rows_here.append(w[layer, 9 * dx + 3 * dy + dz])
                rows_here.append(jnp.zeros((64, 64), BF16))
            wf[layer, dx * 64:(dx + 1) * 64, :] = jnp.concatenate(rows_here, axis=1)
        wf[layer, 192:256, :] = jnp.zeros((64, 768), BF16)

    def build_wb(layer):
        for dy in range(3):
            for dz in range(3):
                row = dy * 256 + dz * 64
                parts = [w[layer, 26 - (9 * dx + 3 * dy + dz)] for dx in range(3)]
                parts.append(jnp.zeros((64, 64), BF16))
                wb[layer - 1, row:row + 64, :] = jnp.concatenate(parts, axis=1)
            wb[layer - 1, dy * 256 + 192:dy * 256 + 256, :] = jnp.zeros((64, 256), BF16)

    def copies(e):
        made = []
        for k, (dr, dc) in enumerate(DIRS):
            if dc == 0:
                s = 0 if dr > 0 else 1
                src, dst = px[e].at[s, pl.ds(0, 4)], px[e].at[s, pl.ds(4, 4)]
            elif dr == 0:
                s = 0 if dc > 0 else 1
                src, dst = py[e].at[s, pl.ds(0, 4)], py[e].at[s, pl.ds(4, 4)]
            else:
                q = (0 if dr > 0 else 1) * 2 + (0 if dc > 0 else 1)
                src, dst = sd[e].at[q], pd[e].at[q]
            copy = (
                pltpu.make_async_remote_copy(
                    src_ref=src, dst_ref=dst, send_sem=send_sem.at[e, k],
                    recv_sem=recv_sem.at[e, k], device_id=peer(dr, dc), device_id_type=MESH,
                )
            )
            made.append((inside(dr, dc), inside(-dr, -dc), copy))
        return made

    def arrive(e, first, end):
        for sends, receives, copy in copies(e)[first:end]:
            pl.when(sends)(copy.wait_send)
            pl.when(receives)(copy.wait_recv)

    def faces_out(e):
        def one(s, carry):
            for sx in range(2):
                x = 7 if sx == 0 else 0
                face = field[s, pl.ds(x * 8, 8)]
                px[e][sx, s] = pack_cols(face)
                for sy in range(2):
                    y = 7 if sy == 0 else 0
                    corner[sx * 2 + sy, s] = face[y]
            for sy in range(2):
                y = 7 if sy == 0 else 0
                face = jnp.concatenate([field[s, pl.ds(x * 8 + y, 1)] for x in range(8)], axis=0)
                py[e][sy, s] = pack_cols(face)
            return carry

        lax.fori_loop(0, 4, one, 0, unroll=2)
        lane = lane_iota((16, 128))
        for q in range(4):
            low = corner[q, 0:2].reshape(16, 128)
            high = corner[q, 2:4].reshape(16, 128)
            sd[e][q] = jnp.where(lane < 64, low, swap_halves(high)).astype(BF16)

    def send_faces(e):
        for sends, _, copy in copies(e):
            pl.when(sends)(copy.start)

    def at(b, o, which=0):
        return idx[(b * 27 + o) * 3 + which]

    def put(z, p, xs, ys, values):
        both = jnp.concatenate(values, axis=1).astype(BF16)
        zp[z, p, xs, ys] = both.reshape(zp[z, p, xs, ys].shape)

    def inner(z):
        def one(t, carry):
            p, x = t // 8, t % 8
            values = []
            for s in range(2):
                b = 2 * p + s
                take = [field[at(b, 12 + j), pl.ds(x * 8, 8)] for j in range(3)]
                values.append(triple(*take))
            put(z, p, pl.ds(x + 1, 1), pl.ds(1, 8), values)
            return carry

        lax.fori_loop(0, 16, one, 0, unroll=4)

    def halo_x(z, e):
        def one(p, carry):
            for sx in range(2):
                ox, cell = 2 * sx - 1, 9 * sx
                values = []
                for s in range(2):
                    o = 9 * (ox + 1) + 3
                    take = [unpack_cols(px[e][sx, at(2 * p + s, o + j)]) for j in range(3)]
                    values.append(triple(*take))
                put(z, p, pl.ds(cell, 1), pl.ds(1, 8), values)
            return carry

        lax.fori_loop(0, 2, one, 0, unroll=True)

    def halo_y(z, e):
        def one(p, carry):
            for sy in range(2):
                oy, cell = 2 * sy - 1, 9 * sy
                values = []
                for s in range(2):
                    o = 9 + 3 * (oy + 1)
                    take = [unpack_cols(py[e][sy, at(2 * p + s, o + j)]) for j in range(3)]
                    values.append(triple(*take))
                put(z, p, pl.ds(1, 8), pl.ds(cell, 1), values)
            return carry

        lax.fori_loop(0, 2, one, 0, unroll=True)

    def halo_edges(z, e):
        for q in range(4):
            wide = pd[e][q].astype(F32)
            corner[q, 0:2] = wide.reshape(2, 8, 128)
            corner[q, 2:4] = swap_halves(wide).reshape(2, 8, 128)

        def one(p, carry):
            for sx in range(2):
                for sy in range(2):
                    values = []
                    for s in range(2):
                        take = []
                        for j in range(3):
                            o = 18 * sx + 6 * sy + j
                            b = 2 * p + s
                            ix, iy, iq = at(b, o), at(b, o, 1), at(b, o, 2)
                            if sy == 0:
                                from_x = swap_halves(px[e][sx, ix, 16:32].astype(F32)[8:16])
                            else:
                                from_x = px[e][sx, ix, 0:16].astype(F32)[0:8]
                            if sx == 0:
                                from_y = swap_halves(py[e][sy, iy, 16:32].astype(F32)[8:16])
                            else:
                                from_y = py[e][sy, iy, 0:16].astype(F32)[0:8]
                            total = from_x + from_y + corner[sx * 2 + sy, iq]
                            take.append(total.reshape(1, 8, 128))
                        values.append(triple(*take))
                    put(z, p, pl.ds(9 * sx, 1), pl.ds(9 * sy, 1), values)
            return carry

        lax.fori_loop(0, 2, one, 0, unroll=True)

    def multiply(stack, layer, forward, dy=None):
        at_dy = slice(0, 768) if dy is None else slice(dy * 256, dy * 256 + 256)
        if forward:
            return lax.dot_general(
                stack, wf[layer, :, at_dy], (((1,), (1,)), ((), ())), preferred_element_type=F32
            )
        return jnp.dot(stack, wb[layer - 1, at_dy, :], preferred_element_type=F32)

    def over_dx(acc):
        low, high = acc[..., 0:128], acc[..., 128:256]
        blank = jnp.zeros_like(low[0:1])
        left = jnp.concatenate([blank, low[0:7]], axis=0)
        right = jnp.concatenate([high[1:8], blank], axis=0)
        return left + swap_halves(low) + right

    def conv_inner(z, layer, forward):
        def one(p, carry):
            stack = jnp.concatenate(
                [zp[z, p, 1:9, dy:dy + 8].reshape(1024, 256) for dy in range(3)], axis=1
            )
            part[p] = over_dx(multiply(stack, layer, forward).reshape(8, 8, 16, 256))
            return carry

        lax.fori_loop(0, 2, one, 0)

    def conv_planes(z, layer, forward):
        planes = jnp.concatenate(
            [
                jnp.concatenate(
                    [zp[z, p, x, dy:dy + 8].reshape(128, 256) for dy in range(3)], axis=1
                )
                for x in (0, 9)
                for p in range(2)
            ],
            axis=0,
        )
        acc = multiply(planes, layer, forward).reshape(2, 2, 8, 16, 256)
        for p in range(2):
            part[p, 0] += acc[0, p, :, :, 0:128]
            part[p, 7] += acc[1, p, :, :, 128:256]

    def conv_lines(z, layer, forward):
        for cell, dy, y in ((0, 0, 0), (9, 2, 7)):
            lines = jnp.concatenate(
                [zp[z, p, 1:9, cell].reshape(128, 256) for p in range(2)], axis=0
            )
            acc = multiply(lines, layer, forward, dy).reshape(2, 8, 16, 256)
            for p in range(2):
                part[p, :, y] += over_dx(acc[p])

    def finish(e, layer, forward):
        arrive(e, 6, 8)
        halo_x(e, e)
        arrive(e, 4, 6)
        halo_y(e, e)
        conv_lines(e, layer, forward)
        arrive(e, 0, 4)
        halo_edges(e, e)
        conv_planes(e, layer, forward)

    def to_field(p, value):
        value = value.reshape(64, 2, 8, 128)
        for s in range(2):
            field[2 * p + s] = value[:, s]

    def correlate(layer):
        for dy in range(3):
            total = jnp.zeros((192, 256), F32)
            for p in range(2):
                z = zp[layer, p, :, dy:dy + 8].reshape(1280, 256)
                total = total + jnp.dot(d3t[p], z, preferred_element_type=F32)
            raw[dy] = total
        lane = lane_iota((64, 128))
        for dx in range(3):
            at_dx = slice(dx * 64, dx * 64 + 64)
            for dy in range(3):
                mine[layer][dy * 3 + dx] = raw[dy, at_dx, 0:128].astype(BF16)
            pair = jnp.where(
                lane < 64, raw[0, at_dx, 128:256], swap_halves(raw[1, at_dx, 128:256])
            )
            mine[layer][9 + dx] = pair.astype(BF16)
        pair = jnp.where(lane < 64, raw[2, 0:64, 128:256], swap_halves(raw[2, 64:128, 128:256]))
        mine[layer][12] = pair.astype(BF16)
        mine[layer][13] = raw[2, 128:192, 128:256].astype(BF16)

    has_unit = c < UNITS

    def wait_bytes(ref, count, sem):
        part = ref.at[pl.ds(0, count)]
        pltpu.make_async_copy(part, part, sem).wait()

    def sum_copy(layer, phase, src, dst, device):
        return pltpu.make_async_remote_copy(
            src_ref=src, dst_ref=dst, send_sem=sum_send.at[layer, phase],
            recv_sem=sum_recv.at[layer, phase], device_id=device, device_id_type=MESH,
        )

    def over(size, body):
        def one(k, carry):
            body(k)
            return carry

        lax.fori_loop(1, size, one, 0)

    def sum_0(layer):
        def send(k):
            to = lax.rem(c + k, cols)

            @pl.when(to < UNITS)
            def _():
                sum_copy(layer, 0, mine[layer].at[to], from_cols[layer].at[c], (r, to)).start()

        over(cols, send)

    def sum_1(layer):
        @pl.when(has_unit)
        def _():
            wait_bytes(from_cols[layer], cols - 1, sum_recv.at[layer, 0])
            from_cols[layer][c] = mine[layer][c]
            total = from_cols[layer][0].astype(F32)
            for k in range(1, cols):
                total = total + from_cols[layer][k].astype(F32)
            from_rows[layer][r] = total.astype(BF16)

            def send(k):
                to = lax.rem(r + k, rows)
                sum_copy(
                    layer, 1, from_rows[layer].at[r], from_rows[layer].at[r], (to, c)
                ).start()

            over(rows, send)

    def sum_2(layer):
        @pl.when(has_unit)
        def _():
            wait_bytes(from_rows[layer], rows - 1, sum_recv.at[layer, 1])
            total = from_rows[layer][0].astype(F32)
            for k in range(1, rows):
                total = total + from_rows[layer][k].astype(F32)
            full[layer][c] = (total * scale).astype(BF16)

            def send(k):
                to = lax.rem(c + k, cols)
                sum_copy(layer, 2, full[layer].at[c], full[layer].at[c], (r, to)).start()

            over(cols, send)

    def sum_3(layer):
        @pl.when(has_unit)
        def _():
            wait_bytes(full[layer], UNITS - 1, sum_recv.at[layer, 2])

        @pl.when(jnp.logical_not(has_unit))
        def _():
            wait_bytes(full[layer], UNITS, sum_recv.at[layer, 2])

        grads[layer] = full[layer][...]

    def sum_end(layer):
        @pl.when(has_unit)
        def _():
            wait_bytes(mine[layer], UNITS - 1, sum_send.at[layer, 0])
            wait_bytes(from_rows[layer], rows - 1, sum_send.at[layer, 1])
            wait_bytes(from_cols[layer], cols - 1, sum_send.at[layer, 2])

        @pl.when(jnp.logical_not(has_unit))
        def _():
            wait_bytes(mine[layer], UNITS, sum_send.at[layer, 0])

    def spread(p, delta):
        lane = lane_iota((10, 8, 16, 128))
        zeros = jnp.zeros((2, 8, 16, 128), F32)
        wide = jnp.concatenate([zeros, delta, zeros], axis=0)
        first = jnp.where(lane < 64, wide[2:12], swap_halves(wide[1:11]))
        second = jnp.where(lane < 64, wide[0:10], 0.0)
        both = jnp.concatenate([first, second], axis=3).reshape(1280, 256)
        d3t[p] = both.astype(BF16).T[0:192]

    def fill_idx(b, carry):
        for o in range(27):
            ox, oy = o // 9 - 1, o // 3 % 3 - 1
            n = nbr[b, o]
            there = n >= 0
            n = jnp.maximum(n, 0)
            slot = n & 3
            dev = n >> 2
            same_r, same_c = (dev // cols) == r, (dev % cols) == c
            base = (b * 27 + o) * 3
            if ox == 0 and oy == 0:
                idx[base] = jnp.where(there, slot, 4)
            elif oy == 0:
                idx[base] = jnp.where(there, slot + jnp.where(same_r, 0, 4), 8)
            elif ox == 0:
                idx[base] = jnp.where(there, slot + jnp.where(same_c, 0, 4), 8)
            else:
                idx[base] = jnp.where(there & same_c, slot + jnp.where(same_r, 0, 4), 8)
                idx[base + 1] = jnp.where(
                    there & same_r & jnp.logical_not(same_c), slot + 4, 8
                )
                idx[base + 2] = jnp.where(
                    there & jnp.logical_not(same_r) & jnp.logical_not(same_c), slot, 4
                )
        return carry

    def prepare():
        lax.fori_loop(0, 4, fill_idx, 0)

        field[4] = jnp.zeros((64, 8, 128), F32)
        for e in range(5):
            for s in range(2):
                px[e][s, 8] = jnp.zeros((32, 128), BF16)
                py[e][s, 8] = jnp.zeros((32, 128), BF16)
            for p in range(2):
                for y in (0, 9):
                    zp[e, p, 1:9, y] = jnp.zeros((8, 16, 256), BF16)
        for q in range(4):
            corner[q, 4] = jnp.zeros((8, 128), F32)

    load_field()
    faces_out(0)
    pl.semaphore_wait(barrier, greeted)
    send_faces(0)
    prepare()
    inner(0)
    fetch_w.wait()
    build_wf(0)
    conv_inner(0, 0, True)
    for layer in (1, 2):
        build_wf(layer)
        build_wb(layer)

    for layer in range(LAYERS):
        if layer > 0:
            faces_out(layer)
            send_faces(layer)
            inner(layer)
            conv_inner(layer, layer, True)
        if layer == 1:
            fetch_cot.wait()
            load_top()
        finish(layer, layer, True)

        def forward(p, carry):
            value = part[p]
            slope = sigmoid(value)
            act = (value * slope).astype(BF16).astype(F32)
            if layer < 2:
                pre[layer, p] = value
                to_field(p, act)
            else:
                last[p] = act.reshape(64, 2, 8, 128)
                slope = slope * (1.0 + value * (1.0 - slope))
                delta = (top[p].reshape(8, 8, 16, 128) * slope).astype(BF16).astype(F32)
                part[p] = delta
                to_field(p, delta)
            return carry

        lax.fori_loop(0, 2, forward, 0)

    def store_out():
        def one(p, carry):
            for s in range(2):
                out[2 * p + s] = last[p, :, s].reshape(512, 128).T[0:64].astype(BF16)
            return carry

        lax.fori_loop(0, 2, one, 0)

    def make_delta(layer, p, grad):
        v = pre[layer, p]
        s = sigmoid(v)
        delta = (grad * (s * (1.0 + v * (1.0 - s)))).astype(BF16).astype(F32)
        part[p] = delta
        to_field(p, delta)

    def spread_all():
        def one(p, carry):
            spread(p, part[p])
            return carry

        lax.fori_loop(0, 2, one, 0)

    for layer in (2, 1):
        e = 5 - layer
        faces_out(e)
        send_faces(e)
        spread_all()
        inner(e)
        conv_inner(e, layer, False)
        correlate(layer)
        sum_0(layer)
        finish(e, layer, False)

        def backward(p, carry):
            make_delta(layer - 1, p, part[p].astype(BF16).astype(F32))
            return carry

        lax.fori_loop(0, 2, backward, 0)
    spread_all()
    correlate(0)
    sum_0(0)
    sum_1(2)
    sum_1(1)
    store_out()
    sum_2(2)
    sum_2(1)
    sum_1(0)
    sum_2(0)
    for layer in (2, 1, 0):
        sum_3(layer)
    for layer in range(LAYERS):
        sum_end(layer)


def write_kernel(act, units, out, grads):
    @pl.when(pl.program_id(0) == 0)
    def _():
        out[...] = act[...]

    for unit, pair in enumerate(UNIT_KERNELS):
        value = units[0, unit].astype(F32)
        grads[0, pair[0]] = value[:, 0:64]
        if len(pair) > 1:
            grads[0, pair[1]] = swap_halves(value)[:, 0:64]


def local(features, weights, cotangent, neighbours):
    rows, cols = lax.axis_size("tx"), lax.axis_size("ty")
    vmem = pl.BlockSpec(memory_space=pltpu.VMEM)
    hbm = pl.BlockSpec(memory_space=pltpu.HBM)
    act, units = pl.pallas_call(
        functools.partial(kernel, rows, cols, 1.0 / math.sqrt(4 * rows * cols * BLK**3)),
        out_shape=(
            jax.ShapeDtypeStruct((4, 64, 512), BF16),
            jax.ShapeDtypeStruct((LAYERS, UNITS, 64, 128), BF16),
        ),
        in_specs=[vmem, hbm, hbm, pl.BlockSpec(memory_space=pltpu.SMEM)],
        out_specs=(vmem, vmem),
        scratch_shapes=[
            pltpu.SMEM((4 * 27 * 3,), jnp.int32),
            pltpu.VMEM((5, 64, 8, 128), F32),
            pltpu.VMEM((5, 2, 10, 10, 16, 256), BF16),
            pltpu.VMEM((2, 2, 8, 8, 16, 128), F32),
            pltpu.VMEM((3, 256, 768), BF16),
            pltpu.VMEM((2, 768, 256), BF16),
            pltpu.VMEM((2, 192, 1280), BF16),
            pltpu.VMEM((3, 192, 256), F32),
            pltpu.VMEM((2, 8, 8, 16, 128), F32),
            pltpu.VMEM((4, 5, 8, 128), F32),
            pltpu.VMEM((2, 64, 2, 8, 128), F32),
            pltpu.VMEM((2, 64, 2, 8, 128), F32),
            pltpu.VMEM((LAYERS, 27, 64, 64), BF16),
            pltpu.VMEM((4, 64, 512), BF16),
            pltpu.SemaphoreType.DMA((2,)),
            pltpu.SemaphoreType.DMA((5, 8)),
            pltpu.SemaphoreType.DMA((5, 8)),
            pltpu.SemaphoreType.DMA((LAYERS, 3)),
            pltpu.SemaphoreType.DMA((LAYERS, 3)),
        ]
        + [pltpu.VMEM((2, 9, 32, 128), BF16)] * 10
        + [pltpu.VMEM((4, 16, 128), BF16)] * 5
        + [pltpu.VMEM((4, 16, 128), BF16)] * 5
        + [pltpu.VMEM((UNITS, 64, 128), BF16)] * LAYERS
        + [pltpu.VMEM((cols, 64, 128), BF16)] * LAYERS
        + [pltpu.VMEM((rows, 64, 128), BF16)] * LAYERS
        + [pltpu.VMEM((UNITS, 64, 128), BF16)] * LAYERS,
        compiler_params=pltpu.CompilerParams(
            collective_id=0, has_side_effects=True, vmem_limit_bytes=56 * 1024 * 1024
        ),
    )(features, weights, cotangent, neighbours)
    return pl.pallas_call(
        write_kernel,
        out_shape=(
            jax.ShapeDtypeStruct((4, 64, 512), BF16),
            jax.ShapeDtypeStruct((LAYERS, 27, 64, 64), F32),
        ),
        grid=(LAYERS,),
        in_specs=[
            pl.BlockSpec((4, 64, 512), lambda layer: (0, 0, 0)),
            pl.BlockSpec((1, UNITS, 64, 128), lambda layer: (layer, 0, 0, 0)),
        ],
        out_specs=(
            pl.BlockSpec((4, 64, 512), lambda layer: (0, 0, 0)),
            pl.BlockSpec((1, 27, 64, 64), lambda layer: (layer, 0, 0, 0)),
        ),
        compiler_params=pltpu.CompilerParams(vmem_limit_bytes=56 * 1024 * 1024),
    )(act, units)


def solution(mesh):
    placed = (P(("tx", "ty"), None, None), P(), P(("tx", "ty"), None, None), P(("tx", "ty"), None))
    return jax.shard_map(
        local,
        mesh=mesh,
        in_specs=placed,
        out_specs=(P(("tx", "ty"), None, None), P()),
        check_vma=False,
    )
```

```python
import functools
import math

import jax
import jax.numpy as jnp
from jax import lax
from jax.experimental import pallas as pl
from jax.experimental.pallas import tpu as pltpu
from jax.sharding import PartitionSpec as P

BLK = 8
LAYERS = 3
F32 = jnp.float32
BF16 = jnp.bfloat16
MESH = pl.DeviceIdType.MESH
DIRS = [(-1, -1), (-1, 1), (1, -1), (1, 1), (0, -1), (0, 1), (-1, 0), (1, 0)]
UNIT_KERNELS = (
    [(9 * dx + 3 * dy, 9 * dx + 3 * dy + 1) for dy in range(3) for dx in range(3)]
    + [(9 * dx + 2, 9 * dx + 5) for dx in range(3)]
    + [(8, 17), (26,)]
)
UNITS = len(UNIT_KERNELS)


def lane_iota(shape):
    return lax.broadcasted_iota(jnp.int32, shape, len(shape) - 1)


def swap_halves(value):
    return pltpu.roll(value, 64, len(value.shape) - 1)


def pack_cols(face):
    low, high = face[0:4], face[4:8]
    packed = jnp.where(lane_iota(low.shape) < 64, low, swap_halves(high))
    return packed.reshape(32, 128).astype(BF16)


def unpack_cols(packed):
    wide = packed.astype(F32).reshape(4, 8, 128)
    return jnp.concatenate([wide, swap_halves(wide)], axis=0)


def triple(below, here, above):
    z = lax.broadcasted_iota(jnp.int32, here.shape, 1)
    lane = lane_iota(here.shape)
    down = pltpu.roll(jnp.where(z == 7, below, here), 1, 1)
    up = pltpu.roll(jnp.where(z == 0, above, here), 7, 1)
    first = jnp.where(lane < 64, down, swap_halves(here))
    second = jnp.where(lane < 64, up, 0.0)
    return jnp.concatenate([first, second], axis=2)


def sigmoid(value):
    return 0.5 + 0.5 * jnp.tanh(0.5 * value)


def kernel(
    rows, cols, scale, feat, w_hbm, cot_hbm, nbr, out, grads,
    idx, field, zp, pre, wf, wb, d3t, raw, part, corner, last, top, w, cot, held,
    fetch_sem, store_sem,
    send_sem, recv_sem, sum_send, sum_recv, *pools,
):
    px, py, pd, sd = pools[0:5], pools[5:10], pools[10:15], pools[15:20]
    mine, from_cols, from_rows, full = (pools[20 + 3 * n:23 + 3 * n] for n in range(4))
    r, c = lax.axis_index("tx"), lax.axis_index("ty")

    def peer(dr, dc):
        return (lax.rem(r + dr + rows, rows), lax.rem(c + dc + cols, cols))

    def inside(dr, dc):
        return (r + dr >= 0) & (r + dr < rows) & (c + dc >= 0) & (c + dc < cols)

    barrier = pltpu.get_barrier_semaphore()
    greeted = rows - 1 + cols - 1
    for dr, dc in DIRS[:4]:
        greeted = greeted + inside(dr, dc).astype(jnp.int32)

        @pl.when(inside(dr, dc))
        def _():
            pl.semaphore_signal(barrier, inc=1, device_id=peer(dr, dc), device_id_type=MESH)

    for dr, dc in [(0, k) for k in range(1, cols)] + [(k, 0) for k in range(1, rows)]:
        pl.semaphore_signal(barrier, inc=1, device_id=peer(dr, dc), device_id_type=MESH)

    fetch_w = pltpu.make_async_copy(w_hbm, w, fetch_sem.at[0])
    fetch_cot = pltpu.make_async_copy(cot_hbm, cot, fetch_sem.at[1])
    fetch_w.start()
    fetch_cot.start()

    def in_rows(block):
        wide = block.astype(F32)
        wide = jnp.concatenate([wide, jnp.zeros((64, 512), F32)], axis=0)
        return wide.T.reshape(64, 8, 128)

    def load_field():
        def one(s, carry):
            field[s] = in_rows(feat[s])
            return carry

        lax.fori_loop(0, 4, one, 0)

    def load_top():
        def one(p, carry):
            for s in range(2):
                top[p, :, :, 8 * s:8 * s + 8, :] = in_rows(cot[2 * p + s]).reshape(8, 8, 8, 128)
            return carry

        lax.fori_loop(0, 2, one, 0)

    def build_wf(layer):
        for dx in range(3):
            rows_here = []
            for dy in range(3):
                for dz in range(3):
                    rows_here.append(w[layer, 9 * dx + 3 * dy + dz])
                rows_here.append(jnp.zeros((64, 64), BF16))
            wf[layer, dx * 64:(dx + 1) * 64, :] = jnp.concatenate(rows_here, axis=1)
        wf[layer, 192:256, :] = jnp.zeros((64, 768), BF16)

    def build_wb(layer):
        for dy in range(3):
            for dz in range(3):
                row = dy * 256 + dz * 64
                parts = [w[layer, 26 - (9 * dx + 3 * dy + dz)] for dx in range(3)]
                parts.append(jnp.zeros((64, 64), BF16))
                wb[layer - 1, row:row + 64, :] = jnp.concatenate(parts, axis=1)
            wb[layer - 1, dy * 256 + 192:dy * 256 + 256, :] = jnp.zeros((64, 256), BF16)

    def copies(e):
        made = []
        for k, (dr, dc) in enumerate(DIRS):
            if dc == 0:
                s = 0 if dr > 0 else 1
                src, dst = px[e].at[s, pl.ds(0, 4)], px[e].at[s, pl.ds(4, 4)]
            elif dr == 0:
                s = 0 if dc > 0 else 1
                src, dst = py[e].at[s, pl.ds(0, 4)], py[e].at[s, pl.ds(4, 4)]
            else:
                q = (0 if dr > 0 else 1) * 2 + (0 if dc > 0 else 1)
                src, dst = sd[e].at[q], pd[e].at[q]
            copy = (
                pltpu.make_async_remote_copy(
                    src_ref=src, dst_ref=dst, send_sem=send_sem.at[e, k],
                    recv_sem=recv_sem.at[e, k], device_id=peer(dr, dc), device_id_type=MESH,
                )
            )
            made.append((inside(dr, dc), inside(-dr, -dc), copy))
        return made

    def arrive(e, first, end):
        for sends, receives, copy in copies(e)[first:end]:
            pl.when(sends)(copy.wait_send)
            pl.when(receives)(copy.wait_recv)

    def pack_corners(e):
        lane = lane_iota((16, 128))
        for q in range(4):
            low = corner[q, 0:2].reshape(16, 128)
            high = corner[q, 2:4].reshape(16, 128)
            sd[e][q] = jnp.where(lane < 64, low, swap_halves(high)).astype(BF16)

    def faces_out(e):
        def one(s, carry):
            for sx in range(2):
                x = 7 if sx == 0 else 0
                face = field[s, pl.ds(x * 8, 8)]
                px[e][sx, s] = pack_cols(face)
                for sy in range(2):
                    y = 7 if sy == 0 else 0
                    corner[sx * 2 + sy, s] = face[y]
            for sy in range(2):
                y = 7 if sy == 0 else 0
                face = jnp.concatenate([field[s, pl.ds(x * 8 + y, 1)] for x in range(8)], axis=0)
                py[e][sy, s] = pack_cols(face)
            return carry

        lax.fori_loop(0, 4, one, 0, unroll=2)
        pack_corners(e)

    def edge_faces(e, point):
        for p in range(2):
            for sx in range(2):
                plane = point(p, (0, 7)[1 - sx]).reshape(8, 2, 8, 128)
                for s in range(2):
                    px[e][sx, 2 * p + s] = pack_cols(plane[:, s])
                    for sy in range(2):
                        corner[sx * 2 + sy, 2 * p + s] = plane[(0, 7)[1 - sy], s]
            for sy in range(2):
                plane = point(p, (slice(0, 8), (0, 7)[1 - sy])).reshape(8, 2, 8, 128)
                for s in range(2):
                    py[e][sy, 2 * p + s] = pack_cols(plane[:, s])
        pack_corners(e)

    def send_faces(e):
        for sends, _, copy in copies(e):
            pl.when(sends)(copy.start)

    def at(b, o, which=0):
        return idx[(b * 27 + o) * 3 + which]

    def put(z, p, xs, ys, values):
        both = jnp.concatenate(values, axis=1).astype(BF16)
        zp[z, p, xs, ys] = both.reshape(zp[z, p, xs, ys].shape)

    def inner(z):
        def one(t, carry):
            p, x = t // 8, t % 8
            values = []
            for s in range(2):
                b = 2 * p + s
                take = [field[at(b, 12 + j), pl.ds(x * 8, 8)] for j in range(3)]
                values.append(triple(*take))
            put(z, p, pl.ds(x + 1, 1), pl.ds(1, 8), values)
            return carry

        lax.fori_loop(0, 16, one, 0, unroll=4)

    def halo_x(z, e):
        def one(p, carry):
            for sx in range(2):
                ox, cell = 2 * sx - 1, 9 * sx
                values = []
                for s in range(2):
                    o = 9 * (ox + 1) + 3
                    take = [unpack_cols(px[e][sx, at(2 * p + s, o + j)]) for j in range(3)]
                    values.append(triple(*take))
                put(z, p, pl.ds(cell, 1), pl.ds(1, 8), values)
            return carry

        lax.fori_loop(0, 2, one, 0, unroll=True)

    def halo_y(z, e):
        def one(p, carry):
            for sy in range(2):
                oy, cell = 2 * sy - 1, 9 * sy
                values = []
                for s in range(2):
                    o = 9 + 3 * (oy + 1)
                    take = [unpack_cols(py[e][sy, at(2 * p + s, o + j)]) for j in range(3)]
                    values.append(triple(*take))
                put(z, p, pl.ds(1, 8), pl.ds(cell, 1), values)
            return carry

        lax.fori_loop(0, 2, one, 0, unroll=True)

    def halo_edges(z, e):
        for q in range(4):
            wide = pd[e][q].astype(F32)
            corner[q, 0:2] = wide.reshape(2, 8, 128)
            corner[q, 2:4] = swap_halves(wide).reshape(2, 8, 128)

        def one(p, carry):
            for sx in range(2):
                for sy in range(2):
                    values = []
                    for s in range(2):
                        take = []
                        for j in range(3):
                            o = 18 * sx + 6 * sy + j
                            b = 2 * p + s
                            ix, iy, iq = at(b, o), at(b, o, 1), at(b, o, 2)
                            if sy == 0:
                                from_x = swap_halves(px[e][sx, ix, 16:32].astype(F32)[8:16])
                            else:
                                from_x = px[e][sx, ix, 0:16].astype(F32)[0:8]
                            if sx == 0:
                                from_y = swap_halves(py[e][sy, iy, 16:32].astype(F32)[8:16])
                            else:
                                from_y = py[e][sy, iy, 0:16].astype(F32)[0:8]
                            total = from_x + from_y + corner[sx * 2 + sy, iq]
                            take.append(total.reshape(1, 8, 128))
                        values.append(triple(*take))
                    put(z, p, pl.ds(9 * sx, 1), pl.ds(9 * sy, 1), values)
            return carry

        lax.fori_loop(0, 2, one, 0, unroll=True)

    def multiply(stack, layer, forward, dy=None):
        at_dy = slice(0, 768) if dy is None else slice(dy * 256, dy * 256 + 256)
        if forward:
            return lax.dot_general(
                stack, wf[layer, :, at_dy], (((1,), (1,)), ((), ())), preferred_element_type=F32
            )
        return jnp.dot(stack, wb[layer - 1, at_dy, :], preferred_element_type=F32)

    def over_dx(acc):
        low, high = acc[..., 0:128], acc[..., 128:256]
        blank = jnp.zeros_like(low[0:1])
        left = jnp.concatenate([blank, low[0:7]], axis=0)
        right = jnp.concatenate([high[1:8], blank], axis=0)
        return left + swap_halves(low) + right

    def conv_inner(z, layer, forward):
        def one(p, carry):
            stack = jnp.concatenate(
                [zp[z, p, 1:9, dy:dy + 8].reshape(1024, 256) for dy in range(3)], axis=1
            )
            part[p] = over_dx(multiply(stack, layer, forward).reshape(8, 8, 16, 256))
            return carry

        lax.fori_loop(0, 2, one, 0)

    def conv_planes(z, layer, forward):
        planes = jnp.concatenate(
            [
                jnp.concatenate(
                    [zp[z, p, x, dy:dy + 8].reshape(128, 256) for dy in range(3)], axis=1
                )
                for x in (0, 9)
                for p in range(2)
            ],
            axis=0,
        )
        acc = multiply(planes, layer, forward).reshape(2, 2, 8, 16, 256)
        for p in range(2):
            part[p, 0] += acc[0, p, :, :, 0:128]
            part[p, 7] += acc[1, p, :, :, 128:256]

    def conv_lines(z, layer, forward):
        for cell, dy, y in ((0, 0, 0), (9, 2, 7)):
            lines = jnp.concatenate(
                [zp[z, p, 1:9, cell].reshape(128, 256) for p in range(2)], axis=0
            )
            acc = multiply(lines, layer, forward, dy).reshape(2, 8, 16, 256)
            for p in range(2):
                part[p, :, y] += over_dx(acc[p])

    def finish(e, layer, forward):
        arrive(e, 6, 8)
        halo_x(e, e)
        arrive(e, 4, 6)
        halo_y(e, e)
        conv_lines(e, layer, forward)
        arrive(e, 0, 4)
        halo_edges(e, e)
        conv_planes(e, layer, forward)

    def to_field(p, value):
        value = value.reshape(64, 2, 8, 128)
        for s in range(2):
            field[2 * p + s] = value[:, s]

    def correlate(layer):
        for dy in range(3):
            total = jnp.zeros((192, 256), F32)
            for p in range(2):
                z = zp[layer, p, :, dy:dy + 8].reshape(1280, 256)
                total = total + jnp.dot(d3t[p], z, preferred_element_type=F32)
            raw[dy] = total
        lane = lane_iota((64, 128))
        for dx in range(3):
            at_dx = slice(dx * 64, dx * 64 + 64)
            for dy in range(3):
                mine[layer][dy * 3 + dx] = raw[dy, at_dx, 0:128].astype(BF16)
            pair = jnp.where(
                lane < 64, raw[0, at_dx, 128:256], swap_halves(raw[1, at_dx, 128:256])
            )
            mine[layer][9 + dx] = pair.astype(BF16)
        pair = jnp.where(lane < 64, raw[2, 0:64, 128:256], swap_halves(raw[2, 64:128, 128:256]))
        mine[layer][12] = pair.astype(BF16)
        mine[layer][13] = raw[2, 128:192, 128:256].astype(BF16)

    has_unit = c < UNITS

    def wait_bytes(ref, count, sem):
        part = ref.at[pl.ds(0, count)]
        pltpu.make_async_copy(part, part, sem).wait()

    def sum_copy(layer, phase, src, dst, device):
        return pltpu.make_async_remote_copy(
            src_ref=src, dst_ref=dst, send_sem=sum_send.at[layer, phase],
            recv_sem=sum_recv.at[layer, phase], device_id=device, device_id_type=MESH,
        )

    def over(size, body):
        def one(k, carry):
            body(k)
            return carry

        lax.fori_loop(1, size, one, 0)

    def sum_0(layer):
        def send(k):
            to = lax.rem(c + k, cols)

            @pl.when(to < UNITS)
            def _():
                sum_copy(layer, 0, mine[layer].at[to], from_cols[layer].at[c], (r, to)).start()

        over(cols, send)

    def sum_1(layer):
        @pl.when(has_unit)
        def _():
            wait_bytes(from_cols[layer], cols - 1, sum_recv.at[layer, 0])
            from_cols[layer][c] = mine[layer][c]
            total = from_cols[layer][0].astype(F32)
            for k in range(1, cols):
                total = total + from_cols[layer][k].astype(F32)
            from_rows[layer][r] = total.astype(BF16)

            def send(k):
                to = lax.rem(r + k, rows)
                sum_copy(
                    layer, 1, from_rows[layer].at[r], from_rows[layer].at[r], (to, c)
                ).start()

            over(rows, send)

    def sum_2(layer):
        @pl.when(has_unit)
        def _():
            wait_bytes(from_rows[layer], rows - 1, sum_recv.at[layer, 1])
            total = from_rows[layer][0].astype(F32)
            for k in range(1, rows):
                total = total + from_rows[layer][k].astype(F32)
            full[layer][c] = (total * scale).astype(BF16)

            def send(k):
                to = lax.rem(c + k, cols)
                sum_copy(layer, 2, full[layer].at[c], full[layer].at[c], (r, to)).start()

            over(cols, send)

    def write_sum(layer):
        return pltpu.make_async_copy(full[layer], grads.at[layer], store_sem.at[layer])

    def sum_3(layer):
        @pl.when(has_unit)
        def _():
            wait_bytes(full[layer], UNITS - 1, sum_recv.at[layer, 2])

        @pl.when(jnp.logical_not(has_unit))
        def _():
            wait_bytes(full[layer], UNITS, sum_recv.at[layer, 2])

        write_sum(layer).start()

    def sum_end(layer):
        @pl.when(has_unit)
        def _():
            wait_bytes(mine[layer], UNITS - 1, sum_send.at[layer, 0])
            wait_bytes(from_rows[layer], rows - 1, sum_send.at[layer, 1])
            wait_bytes(from_cols[layer], cols - 1, sum_send.at[layer, 2])

        @pl.when(jnp.logical_not(has_unit))
        def _():
            wait_bytes(mine[layer], UNITS, sum_send.at[layer, 0])

    def spread(p, delta):
        lane = lane_iota((10, 8, 16, 128))
        zeros = jnp.zeros((2, 8, 16, 128), F32)
        wide = jnp.concatenate([zeros, delta, zeros], axis=0)
        first = jnp.where(lane < 64, wide[2:12], swap_halves(wide[1:11]))
        second = jnp.where(lane < 64, wide[0:10], 0.0)
        both = jnp.concatenate([first, second], axis=3).reshape(1280, 256)
        d3t[p] = both.astype(BF16).T[0:192]

    def fill_idx(b, carry):
        for o in range(27):
            ox, oy = o // 9 - 1, o // 3 % 3 - 1
            n = nbr[b, o]
            there = n >= 0
            n = jnp.maximum(n, 0)
            slot = n & 3
            dev = n >> 2
            same_r, same_c = (dev // cols) == r, (dev % cols) == c
            base = (b * 27 + o) * 3
            if ox == 0 and oy == 0:
                idx[base] = jnp.where(there, slot, 4)
            elif oy == 0:
                idx[base] = jnp.where(there, slot + jnp.where(same_r, 0, 4), 8)
            elif ox == 0:
                idx[base] = jnp.where(there, slot + jnp.where(same_c, 0, 4), 8)
            else:
                idx[base] = jnp.where(there & same_c, slot + jnp.where(same_r, 0, 4), 8)
                idx[base + 1] = jnp.where(
                    there & same_r & jnp.logical_not(same_c), slot + 4, 8
                )
                idx[base + 2] = jnp.where(
                    there & jnp.logical_not(same_r) & jnp.logical_not(same_c), slot, 4
                )
        return carry

    def prepare():
        lax.fori_loop(0, 4, fill_idx, 0)

        field[4] = jnp.zeros((64, 8, 128), F32)
        for e in range(5):
            for s in range(2):
                px[e][s, 8] = jnp.zeros((32, 128), BF16)
                py[e][s, 8] = jnp.zeros((32, 128), BF16)
            for p in range(2):
                for y in (0, 9):
                    zp[e, p, 1:9, y] = jnp.zeros((8, 16, 256), BF16)
        for q in range(4):
            corner[q, 4] = jnp.zeros((8, 128), F32)

    load_field()
    faces_out(0)
    pl.semaphore_wait(barrier, greeted)
    send_faces(0)
    prepare()
    inner(0)
    fetch_w.wait()
    build_wf(0)
    conv_inner(0, 0, True)
    for layer in (1, 2):
        build_wf(layer)
        build_wb(layer)

    def cells(ref, p, where):
        return ref[(p, *where)] if isinstance(where, tuple) else ref[p, where]

    def act_point(p, where):
        value = cells(part, p, where)
        return (value * sigmoid(value)).astype(BF16).astype(F32)

    def slope_of(value):
        s = sigmoid(value)
        return s * (1.0 + value * (1.0 - s))

    def top_point(p, where):
        return (cells(top, p, where) * slope_of(cells(part, p, where))).astype(BF16).astype(F32)

    def delta_point(layer):
        def point(p, where):
            grad = cells(part, p, where).astype(BF16).astype(F32)
            return (grad * slope_of(cells(pre.at[layer], p, where))).astype(BF16).astype(F32)

        return point

    def all_cells(body):
        def one(p, carry):
            body(p)
            return carry

        lax.fori_loop(0, 2, one, 0)

    everywhere = slice(0, 8)

    def whole_act(layer):
        def body(p):
            act = act_point(p, everywhere)
            if layer < 2:
                pre[layer, p] = part[p]
                to_field(p, act)
            else:
                last[p] = act.reshape(64, 2, 8, 128)

        all_cells(body)

    def whole_delta(point):
        def body(p):
            delta = point(p, everywhere)
            part[p] = delta
            to_field(p, delta)

        all_cells(body)

    for layer in range(LAYERS):
        if layer > 0:
            edge_faces(layer, act_point)
            send_faces(layer)
            whole_act(layer - 1)
            inner(layer)
            conv_inner(layer, layer, True)
        if layer == 1:
            fetch_cot.wait()
            load_top()
        finish(layer, layer, True)

    write_out = pltpu.make_async_copy(held, out, store_sem.at[LAYERS])

    def store_out():
        def one(p, carry):
            for s in range(2):
                held[2 * p + s] = last[p, :, s].reshape(512, 128).T[0:64].astype(BF16)
            return carry

        lax.fori_loop(0, 2, one, 0)
        write_out.start()

    def spread_all():
        def one(p, carry):
            spread(p, part[p])
            return carry

        lax.fori_loop(0, 2, one, 0)

    for layer in (2, 1):
        e = 5 - layer
        point = top_point if layer == 2 else delta_point(layer)
        edge_faces(e, point)
        send_faces(e)
        if layer == 2:
            whole_act(2)
        whole_delta(point)
        spread_all()
        inner(e)
        conv_inner(e, layer, False)
        correlate(layer)
        sum_0(layer)
        finish(e, layer, False)

    def last_delta(p):
        part[p] = delta_point(0)(p, everywhere)

    all_cells(last_delta)
    spread_all()
    correlate(0)
    sum_0(0)
    sum_1(2)
    sum_1(1)
    store_out()
    sum_2(2)
    sum_2(1)
    sum_1(0)
    sum_2(0)
    for layer in (2, 1, 0):
        sum_3(layer)
    for layer in range(LAYERS):
        sum_end(layer)
        write_sum(layer).wait()
    write_out.wait()


def write_kernel(act, units, out, grads, held, units_in, wide, sems):
    fetch_act = pltpu.make_async_copy(act, held, sems.at[0])
    store_act = pltpu.make_async_copy(held, out, sems.at[1])
    fetch = [
        pltpu.make_async_copy(units.at[layer], units_in.at[layer], sems.at[2 + layer])
        for layer in range(LAYERS)
    ]
    store = [
        pltpu.make_async_copy(wide.at[layer], grads.at[layer], sems.at[2 + LAYERS + layer])
        for layer in range(LAYERS)
    ]
    for copy in fetch:
        copy.start()
    fetch_act.start()
    for layer in range(LAYERS):
        fetch[layer].wait()
        for unit, pair in enumerate(UNIT_KERNELS):
            value = units_in[layer, unit].astype(F32)
            wide[layer, pair[0]] = value[:, 0:64]
            if len(pair) > 1:
                wide[layer, pair[1]] = swap_halves(value)[:, 0:64]
        store[layer].start()
        if layer == 0:
            fetch_act.wait()
            store_act.start()
    for copy in store:
        copy.wait()
    store_act.wait()


def local(features, weights, cotangent, neighbours):
    rows, cols = lax.axis_size("tx"), lax.axis_size("ty")
    vmem = pl.BlockSpec(memory_space=pltpu.VMEM)
    hbm = pl.BlockSpec(memory_space=pltpu.HBM)
    act, units = pl.pallas_call(
        functools.partial(kernel, rows, cols, 1.0 / math.sqrt(4 * rows * cols * BLK**3)),
        out_shape=(
            jax.ShapeDtypeStruct((4, 64, 512), BF16),
            jax.ShapeDtypeStruct((LAYERS, UNITS, 64, 128), BF16),
        ),
        in_specs=[vmem, hbm, hbm, pl.BlockSpec(memory_space=pltpu.SMEM)],
        out_specs=(hbm, hbm),
        scratch_shapes=[
            pltpu.SMEM((4 * 27 * 3,), jnp.int32),
            pltpu.VMEM((5, 64, 8, 128), F32),
            pltpu.VMEM((5, 2, 10, 10, 16, 256), BF16),
            pltpu.VMEM((2, 2, 8, 8, 16, 128), F32),
            pltpu.VMEM((3, 256, 768), BF16),
            pltpu.VMEM((2, 768, 256), BF16),
            pltpu.VMEM((2, 192, 1280), BF16),
            pltpu.VMEM((3, 192, 256), F32),
            pltpu.VMEM((2, 8, 8, 16, 128), F32),
            pltpu.VMEM((4, 5, 8, 128), F32),
            pltpu.VMEM((2, 64, 2, 8, 128), F32),
            pltpu.VMEM((2, 8, 8, 16, 128), F32),
            pltpu.VMEM((LAYERS, 27, 64, 64), BF16),
            pltpu.VMEM((4, 64, 512), BF16),
            pltpu.VMEM((4, 64, 512), BF16),
            pltpu.SemaphoreType.DMA((2,)),
            pltpu.SemaphoreType.DMA((LAYERS + 1,)),
            pltpu.SemaphoreType.DMA((5, 8)),
            pltpu.SemaphoreType.DMA((5, 8)),
            pltpu.SemaphoreType.DMA((LAYERS, 3)),
            pltpu.SemaphoreType.DMA((LAYERS, 3)),
        ]
        + [pltpu.VMEM((2, 9, 32, 128), BF16)] * 10
        + [pltpu.VMEM((4, 16, 128), BF16)] * 5
        + [pltpu.VMEM((4, 16, 128), BF16)] * 5
        + [pltpu.VMEM((UNITS, 64, 128), BF16)] * LAYERS
        + [pltpu.VMEM((cols, 64, 128), BF16)] * LAYERS
        + [pltpu.VMEM((rows, 64, 128), BF16)] * LAYERS
        + [pltpu.VMEM((UNITS, 64, 128), BF16)] * LAYERS,
        compiler_params=pltpu.CompilerParams(
            collective_id=0, has_side_effects=True, vmem_limit_bytes=56 * 1024 * 1024
        ),
    )(features, weights, cotangent, neighbours)
    return pl.pallas_call(
        write_kernel,
        out_shape=(
            jax.ShapeDtypeStruct((4, 64, 512), BF16),
            jax.ShapeDtypeStruct((LAYERS, 27, 64, 64), F32),
        ),
        in_specs=[hbm, hbm],
        out_specs=(hbm, hbm),
        scratch_shapes=[
            pltpu.VMEM((4, 64, 512), BF16),
            pltpu.VMEM((LAYERS, UNITS, 64, 128), BF16),
            pltpu.VMEM((LAYERS, 27, 64, 64), F32),
            pltpu.SemaphoreType.DMA((2 + 2 * LAYERS,)),
        ],
        compiler_params=pltpu.CompilerParams(vmem_limit_bytes=56 * 1024 * 1024),
    )(act, units)


def solution(mesh):
    placed = (P(("tx", "ty"), None, None), P(), P(("tx", "ty"), None, None), P(("tx", "ty"), None))
    return jax.shard_map(
        local,
        mesh=mesh,
        in_specs=placed,
        out_specs=(P(("tx", "ty"), None, None), P()),
        check_vma=False,
    )
```

```python
import functools
import math

import jax
import jax.numpy as jnp
from jax import lax
from jax.experimental import pallas as pl
from jax.experimental.pallas import tpu as pltpu
from jax.sharding import PartitionSpec as P

BLK = 8
LAYERS = 3
F32 = jnp.float32
BF16 = jnp.bfloat16
MESH = pl.DeviceIdType.MESH
DIRS = [(-1, -1), (-1, 1), (1, -1), (1, 1), (0, -1), (0, 1), (-1, 0), (1, 0)]
UNIT_KERNELS = (
    [(9 * dx + 3 * dy, 9 * dx + 3 * dy + 1) for dy in range(3) for dx in range(3)]
    + [(9 * dx + 2, 9 * dx + 5) for dx in range(3)]
    + [(8, 17), (26,)]
)
UNITS = len(UNIT_KERNELS)


def lane_iota(shape):
    return lax.broadcasted_iota(jnp.int32, shape, len(shape) - 1)


def swap_halves(value):
    return pltpu.roll(value, 64, len(value.shape) - 1)


def pack_cols(face):
    low, high = face[0:4], face[4:8]
    packed = jnp.where(lane_iota(low.shape) < 64, low, swap_halves(high))
    return packed.reshape(32, 128).astype(BF16)


def unpack_cols(packed):
    wide = packed.astype(F32).reshape(4, 8, 128)
    return jnp.concatenate([wide, swap_halves(wide)], axis=0)


def triple(below, here, above):
    z = lax.broadcasted_iota(jnp.int32, here.shape, 1)
    lane = lane_iota(here.shape)
    down = pltpu.roll(jnp.where(z == 7, below, here), 1, 1)
    up = pltpu.roll(jnp.where(z == 0, above, here), 7, 1)
    first = jnp.where(lane < 64, down, swap_halves(here))
    second = jnp.where(lane < 64, up, 0.0)
    return jnp.concatenate([first, second], axis=2)


def sigmoid(value):
    return 0.5 + 0.5 * jnp.tanh(0.5 * value)


def kernel(
    rows, cols, scale, feat, w_hbm, cot_hbm, nbr, out, grads,
    idx, field, zp, pre, wf, wb, d3t, raw, part, corner, last, top, w, cot, held,
    fetch_sem, store_sem,
    send_sem, recv_sem, sum_send, sum_recv, *pools,
):
    px, py, pd, sd = pools[0:5], pools[5:10], pools[10:15], pools[15:20]
    mine, from_cols, from_rows, full = (pools[20 + 3 * n:23 + 3 * n] for n in range(4))
    r, c = lax.axis_index("tx"), lax.axis_index("ty")

    def peer(dr, dc):
        return (lax.rem(r + dr + rows, rows), lax.rem(c + dc + cols, cols))

    def inside(dr, dc):
        return (r + dr >= 0) & (r + dr < rows) & (c + dc >= 0) & (c + dc < cols)

    barrier = pltpu.get_barrier_semaphore()
    greeted = rows - 1 + cols - 1
    for dr, dc in DIRS[:4]:
        greeted = greeted + inside(dr, dc).astype(jnp.int32)

        @pl.when(inside(dr, dc))
        def _():
            pl.semaphore_signal(barrier, inc=1, device_id=peer(dr, dc), device_id_type=MESH)

    for dr, dc in [(0, k) for k in range(1, cols)] + [(k, 0) for k in range(1, rows)]:
        pl.semaphore_signal(barrier, inc=1, device_id=peer(dr, dc), device_id_type=MESH)

    fetch_w = pltpu.make_async_copy(w_hbm, w, fetch_sem.at[0])
    fetch_cot = pltpu.make_async_copy(cot_hbm, cot, fetch_sem.at[1])
    fetch_w.start()
    fetch_cot.start()

    def in_rows(block):
        wide = block.astype(F32)
        wide = jnp.concatenate([wide, jnp.zeros((64, 512), F32)], axis=0)
        return wide.T.reshape(64, 8, 128)

    def load_field():
        def one(s, carry):
            field[s] = in_rows(feat[s])
            return carry

        lax.fori_loop(0, 4, one, 0)

    def load_top():
        def one(p, carry):
            for s in range(2):
                top[p, :, :, 8 * s:8 * s + 8, :] = in_rows(cot[2 * p + s]).reshape(8, 8, 8, 128)
            return carry

        lax.fori_loop(0, 2, one, 0)

    def build_wf(layer):
        for dx in range(3):
            rows_here = []
            for dy in range(3):
                for dz in range(3):
                    rows_here.append(w[layer, 9 * dx + 3 * dy + dz])
                rows_here.append(jnp.zeros((64, 64), BF16))
            wf[layer, dx * 64:(dx + 1) * 64, :] = jnp.concatenate(rows_here, axis=1)
        wf[layer, 192:256, :] = jnp.zeros((64, 768), BF16)

    def build_wb(layer):
        for dy in range(3):
            for dz in range(3):
                row = dy * 256 + dz * 64
                parts = [w[layer, 26 - (9 * dx + 3 * dy + dz)] for dx in range(3)]
                parts.append(jnp.zeros((64, 64), BF16))
                wb[layer - 1, row:row + 64, :] = jnp.concatenate(parts, axis=1)
            wb[layer - 1, dy * 256 + 192:dy * 256 + 256, :] = jnp.zeros((64, 256), BF16)

    def copies(e):
        made = []
        for k, (dr, dc) in enumerate(DIRS):
            if dc == 0:
                s = 0 if dr > 0 else 1
                src, dst = px[e].at[s, pl.ds(0, 4)], px[e].at[s, pl.ds(4, 4)]
            elif dr == 0:
                s = 0 if dc > 0 else 1
                src, dst = py[e].at[s, pl.ds(0, 4)], py[e].at[s, pl.ds(4, 4)]
            else:
                q = (0 if dr > 0 else 1) * 2 + (0 if dc > 0 else 1)
                src, dst = sd[e].at[q], pd[e].at[q]
            copy = (
                pltpu.make_async_remote_copy(
                    src_ref=src, dst_ref=dst, send_sem=send_sem.at[e, k],
                    recv_sem=recv_sem.at[e, k], device_id=peer(dr, dc), device_id_type=MESH,
                )
            )
            made.append((inside(dr, dc), inside(-dr, -dc), copy))
        return made

    def arrive(e, first, end):
        for sends, receives, copy in copies(e)[first:end]:
            pl.when(sends)(copy.wait_send)
            pl.when(receives)(copy.wait_recv)

    def pack_corners(e):
        lane = lane_iota((16, 128))
        for q in range(4):
            low = corner[q, 0:2].reshape(16, 128)
            high = corner[q, 2:4].reshape(16, 128)
            sd[e][q] = jnp.where(lane < 64, low, swap_halves(high)).astype(BF16)

    def faces_out(e):
        def one(s, carry):
            for sx in range(2):
                x = 7 if sx == 0 else 0
                face = field[s, pl.ds(x * 8, 8)]
                px[e][sx, s] = pack_cols(face)
                for sy in range(2):
                    y = 7 if sy == 0 else 0
                    corner[sx * 2 + sy, s] = face[y]
            for sy in range(2):
                y = 7 if sy == 0 else 0
                face = jnp.concatenate([field[s, pl.ds(x * 8 + y, 1)] for x in range(8)], axis=0)
                py[e][sy, s] = pack_cols(face)
            return carry

        lax.fori_loop(0, 4, one, 0, unroll=2)
        pack_corners(e)

    def edge_faces(e, point):
        for p in range(2):
            for sx in range(2):
                plane = point(p, (0, 7)[1 - sx]).reshape(8, 2, 8, 128)
                for s in range(2):
                    px[e][sx, 2 * p + s] = pack_cols(plane[:, s])
                    for sy in range(2):
                        corner[sx * 2 + sy, 2 * p + s] = plane[(0, 7)[1 - sy], s]
            for sy in range(2):
                plane = point(p, (slice(0, 8), (0, 7)[1 - sy])).reshape(8, 2, 8, 128)
                for s in range(2):
                    py[e][sy, 2 * p + s] = pack_cols(plane[:, s])
        pack_corners(e)

    def send_faces(e):
        for sends, _, copy in copies(e):
            pl.when(sends)(copy.start)

    def at(b, o, which=0):
        return idx[(b * 27 + o) * 3 + which]

    def put(z, p, xs, ys, values):
        both = jnp.concatenate(values, axis=1).astype(BF16)
        zp[z, p, xs, ys] = both.reshape(zp[z, p, xs, ys].shape)

    def inner(z):
        def one(t, carry):
            p, x = t // 8, t % 8
            values = []
            for s in range(2):
                b = 2 * p + s
                take = [field[at(b, 12 + j), pl.ds(x * 8, 8)] for j in range(3)]
                values.append(triple(*take))
            put(z, p, pl.ds(x + 1, 1), pl.ds(1, 8), values)
            return carry

        lax.fori_loop(0, 16, one, 0, unroll=4)

    def halo_x(z, e):
        def one(p, carry):
            for sx in range(2):
                ox, cell = 2 * sx - 1, 9 * sx
                values = []
                for s in range(2):
                    o = 9 * (ox + 1) + 3
                    take = [unpack_cols(px[e][sx, at(2 * p + s, o + j)]) for j in range(3)]
                    values.append(triple(*take))
                put(z, p, pl.ds(cell, 1), pl.ds(1, 8), values)
            return carry

        lax.fori_loop(0, 2, one, 0, unroll=True)

    def halo_y(z, e):
        def one(p, carry):
            for sy in range(2):
                oy, cell = 2 * sy - 1, 9 * sy
                values = []
                for s in range(2):
                    o = 9 + 3 * (oy + 1)
                    take = [unpack_cols(py[e][sy, at(2 * p + s, o + j)]) for j in range(3)]
                    values.append(triple(*take))
                put(z, p, pl.ds(1, 8), pl.ds(cell, 1), values)
            return carry

        lax.fori_loop(0, 2, one, 0, unroll=True)

    def halo_edges(z, e):
        for q in range(4):
            wide = pd[e][q].astype(F32)
            corner[q, 0:2] = wide.reshape(2, 8, 128)
            corner[q, 2:4] = swap_halves(wide).reshape(2, 8, 128)

        def one(p, carry):
            for sx in range(2):
                for sy in range(2):
                    values = []
                    for s in range(2):
                        take = []
                        for j in range(3):
                            o = 18 * sx + 6 * sy + j
                            b = 2 * p + s
                            ix, iy, iq = at(b, o), at(b, o, 1), at(b, o, 2)
                            if sy == 0:
                                from_x = swap_halves(px[e][sx, ix, 16:32].astype(F32)[8:16])
                            else:
                                from_x = px[e][sx, ix, 0:16].astype(F32)[0:8]
                            if sx == 0:
                                from_y = swap_halves(py[e][sy, iy, 16:32].astype(F32)[8:16])
                            else:
                                from_y = py[e][sy, iy, 0:16].astype(F32)[0:8]
                            total = from_x + from_y + corner[sx * 2 + sy, iq]
                            take.append(total.reshape(1, 8, 128))
                        values.append(triple(*take))
                    put(z, p, pl.ds(9 * sx, 1), pl.ds(9 * sy, 1), values)
            return carry

        lax.fori_loop(0, 2, one, 0, unroll=True)

    def multiply(stack, layer, forward, dy=None):
        at_dy = slice(0, 768) if dy is None else slice(dy * 256, dy * 256 + 256)
        if forward:
            return lax.dot_general(
                stack, wf[layer, :, at_dy], (((1,), (1,)), ((), ())), preferred_element_type=F32
            )
        return jnp.dot(stack, wb[layer - 1, at_dy, :], preferred_element_type=F32)

    def over_dx(acc):
        low, high = acc[..., 0:128], acc[..., 128:256]
        blank = jnp.zeros_like(low[0:1])
        left = jnp.concatenate([blank, low[0:7]], axis=0)
        right = jnp.concatenate([high[1:8], blank], axis=0)
        return left + swap_halves(low) + right

    def conv_inner(z, layer, forward):
        def one(p, carry):
            stack = jnp.concatenate(
                [zp[z, p, 1:9, dy:dy + 8].reshape(1024, 256) for dy in range(3)], axis=1
            )
            part[p] = over_dx(multiply(stack, layer, forward).reshape(8, 8, 16, 256))
            return carry

        lax.fori_loop(0, 2, one, 0)

    def conv_planes(z, layer, forward):
        planes = jnp.concatenate(
            [
                jnp.concatenate(
                    [zp[z, p, x, dy:dy + 8].reshape(128, 256) for dy in range(3)], axis=1
                )
                for x in (0, 9)
                for p in range(2)
            ],
            axis=0,
        )
        acc = multiply(planes, layer, forward).reshape(2, 2, 8, 16, 256)
        for p in range(2):
            part[p, 0] += acc[0, p, :, :, 0:128]
            part[p, 7] += acc[1, p, :, :, 128:256]

    def conv_lines(z, layer, forward):
        for cell, dy, y in ((0, 0, 0), (9, 2, 7)):
            lines = jnp.concatenate(
                [zp[z, p, 1:9, cell].reshape(128, 256) for p in range(2)], axis=0
            )
            acc = multiply(lines, layer, forward, dy).reshape(2, 8, 16, 256)
            for p in range(2):
                part[p, :, y] += over_dx(acc[p])

    def conv_corners(z, layer, forward):
        for cell, dy, y in ((0, 0, 0), (9, 2, 7)):
            lines = jnp.concatenate(
                [zp[z, p, x, cell] for x in (0, 9) for p in range(2)], axis=0
            )
            acc = multiply(lines, layer, forward, dy).reshape(2, 2, 16, 256)
            for p in range(2):
                part[p, 0, y] += acc[0, p, :, 0:128]
                part[p, 7, y] += acc[1, p, :, 128:256]

    def finish(e, layer, forward):
        arrive(e, 6, 8)
        halo_x(e, e)
        conv_planes(e, layer, forward)
        arrive(e, 4, 6)
        halo_y(e, e)
        conv_lines(e, layer, forward)
        arrive(e, 0, 4)
        halo_edges(e, e)
        conv_corners(e, layer, forward)

    def to_field(p, value):
        value = value.reshape(64, 2, 8, 128)
        for s in range(2):
            field[2 * p + s] = value[:, s]

    def correlate(layer):
        for dy in range(3):
            total = jnp.zeros((192, 256), F32)
            for p in range(2):
                z = zp[layer, p, :, dy:dy + 8].reshape(1280, 256)
                total = total + jnp.dot(d3t[p], z, preferred_element_type=F32)
            raw[dy] = total
        lane = lane_iota((64, 128))
        for dx in range(3):
            at_dx = slice(dx * 64, dx * 64 + 64)
            for dy in range(3):
                mine[layer][dy * 3 + dx] = raw[dy, at_dx, 0:128].astype(BF16)
            pair = jnp.where(
                lane < 64, raw[0, at_dx, 128:256], swap_halves(raw[1, at_dx, 128:256])
            )
            mine[layer][9 + dx] = pair.astype(BF16)
        pair = jnp.where(lane < 64, raw[2, 0:64, 128:256], swap_halves(raw[2, 64:128, 128:256]))
        mine[layer][12] = pair.astype(BF16)
        mine[layer][13] = raw[2, 128:192, 128:256].astype(BF16)

    has_unit = c < UNITS

    def wait_bytes(ref, count, sem):
        part = ref.at[pl.ds(0, count)]
        pltpu.make_async_copy(part, part, sem).wait()

    def sum_copy(layer, phase, src, dst, device):
        return pltpu.make_async_remote_copy(
            src_ref=src, dst_ref=dst, send_sem=sum_send.at[layer, phase],
            recv_sem=sum_recv.at[layer, phase], device_id=device, device_id_type=MESH,
        )

    def over(size, body):
        def one(k, carry):
            body(k)
            return carry

        lax.fori_loop(1, size, one, 0)

    def sum_0(layer):
        def send(k):
            to = lax.rem(c + k, cols)

            @pl.when(to < UNITS)
            def _():
                sum_copy(layer, 0, mine[layer].at[to], from_cols[layer].at[c], (r, to)).start()

        over(cols, send)

    def sum_1(layer):
        @pl.when(has_unit)
        def _():
            wait_bytes(from_cols[layer], cols - 1, sum_recv.at[layer, 0])
            from_cols[layer][c] = mine[layer][c]
            total = from_cols[layer][0].astype(F32)
            for k in range(1, cols):
                total = total + from_cols[layer][k].astype(F32)
            from_rows[layer][r] = total.astype(BF16)

            def send(k):
                to = lax.rem(r + k, rows)
                sum_copy(
                    layer, 1, from_rows[layer].at[r], from_rows[layer].at[r], (to, c)
                ).start()

            over(rows, send)

    def sum_2(layer):
        @pl.when(has_unit)
        def _():
            wait_bytes(from_rows[layer], rows - 1, sum_recv.at[layer, 1])
            total = from_rows[layer][0].astype(F32)
            for k in range(1, rows):
                total = total + from_rows[layer][k].astype(F32)
            full[layer][c] = (total * scale).astype(BF16)

            def send(k):
                to = lax.rem(c + k, cols)
                sum_copy(layer, 2, full[layer].at[c], full[layer].at[c], (r, to)).start()

            over(cols, send)

    def write_sum(layer):
        return pltpu.make_async_copy(full[layer], grads.at[layer], store_sem.at[layer])

    def sum_3(layer):
        @pl.when(has_unit)
        def _():
            wait_bytes(full[layer], UNITS - 1, sum_recv.at[layer, 2])

        @pl.when(jnp.logical_not(has_unit))
        def _():
            wait_bytes(full[layer], UNITS, sum_recv.at[layer, 2])

        write_sum(layer).start()

    def sum_end(layer):
        @pl.when(has_unit)
        def _():
            wait_bytes(mine[layer], UNITS - 1, sum_send.at[layer, 0])
            wait_bytes(from_rows[layer], rows - 1, sum_send.at[layer, 1])
            wait_bytes(from_cols[layer], cols - 1, sum_send.at[layer, 2])

        @pl.when(jnp.logical_not(has_unit))
        def _():
            wait_bytes(mine[layer], UNITS, sum_send.at[layer, 0])

    def spread(p, delta):
        lane = lane_iota((10, 8, 16, 128))
        zeros = jnp.zeros((2, 8, 16, 128), F32)
        wide = jnp.concatenate([zeros, delta, zeros], axis=0)
        first = jnp.where(lane < 64, wide[2:12], swap_halves(wide[1:11]))
        second = jnp.where(lane < 64, wide[0:10], 0.0)
        both = jnp.concatenate([first, second], axis=3).reshape(1280, 256)
        d3t[p] = both.astype(BF16).T[0:192]

    def fill_idx(b, carry):
        for o in range(27):
            ox, oy = o // 9 - 1, o // 3 % 3 - 1
            n = nbr[b, o]
            there = n >= 0
            n = jnp.maximum(n, 0)
            slot = n & 3
            dev = n >> 2
            same_r, same_c = (dev // cols) == r, (dev % cols) == c
            base = (b * 27 + o) * 3
            if ox == 0 and oy == 0:
                idx[base] = jnp.where(there, slot, 4)
            elif oy == 0:
                idx[base] = jnp.where(there, slot + jnp.where(same_r, 0, 4), 8)
            elif ox == 0:
                idx[base] = jnp.where(there, slot + jnp.where(same_c, 0, 4), 8)
            else:
                idx[base] = jnp.where(there & same_c, slot + jnp.where(same_r, 0, 4), 8)
                idx[base + 1] = jnp.where(
                    there & same_r & jnp.logical_not(same_c), slot + 4, 8
                )
                idx[base + 2] = jnp.where(
                    there & jnp.logical_not(same_r) & jnp.logical_not(same_c), slot, 4
                )
        return carry

    def prepare():
        lax.fori_loop(0, 4, fill_idx, 0)

        field[4] = jnp.zeros((64, 8, 128), F32)
        for e in range(5):
            for s in range(2):
                px[e][s, 8] = jnp.zeros((32, 128), BF16)
                py[e][s, 8] = jnp.zeros((32, 128), BF16)
            for p in range(2):
                for y in (0, 9):
                    zp[e, p, 1:9, y] = jnp.zeros((8, 16, 256), BF16)
                    for x in (0, 9):
                        zp[e, p, x, y] = jnp.zeros((16, 256), BF16)
        for q in range(4):
            corner[q, 4] = jnp.zeros((8, 128), F32)

    load_field()
    faces_out(0)
    pl.semaphore_wait(barrier, greeted)
    send_faces(0)
    prepare()
    inner(0)
    fetch_w.wait()
    build_wf(0)
    conv_inner(0, 0, True)
    for layer in (1, 2):
        build_wf(layer)
        build_wb(layer)

    def cells(ref, p, where):
        return ref[(p, *where)] if isinstance(where, tuple) else ref[p, where]

    def act_point(p, where):
        value = cells(part, p, where)
        return (value * sigmoid(value)).astype(BF16).astype(F32)

    def slope_of(value):
        s = sigmoid(value)
        return s * (1.0 + value * (1.0 - s))

    def top_point(p, where):
        return (cells(top, p, where) * slope_of(cells(part, p, where))).astype(BF16).astype(F32)

    def delta_point(layer):
        def point(p, where):
            grad = cells(part, p, where).astype(BF16).astype(F32)
            return (grad * slope_of(cells(pre.at[layer], p, where))).astype(BF16).astype(F32)

        return point

    def all_cells(body):
        def one(p, carry):
            body(p)
            return carry

        lax.fori_loop(0, 2, one, 0)

    everywhere = slice(0, 8)

    def whole_act(layer):
        def body(p):
            act = act_point(p, everywhere)
            if layer < 2:
                pre[layer, p] = part[p]
                to_field(p, act)
            else:
                last[p] = act.reshape(64, 2, 8, 128)

        all_cells(body)

    def whole_delta(point):
        def body(p):
            delta = point(p, everywhere)
            part[p] = delta
            to_field(p, delta)

        all_cells(body)

    for layer in range(LAYERS):
        if layer > 0:
            edge_faces(layer, act_point)
            send_faces(layer)
            whole_act(layer - 1)
            inner(layer)
            conv_inner(layer, layer, True)
        if layer == 1:
            fetch_cot.wait()
            load_top()
        finish(layer, layer, True)

    write_out = pltpu.make_async_copy(held, out, store_sem.at[LAYERS])

    def store_out():
        def one(p, carry):
            for s in range(2):
                held[2 * p + s] = last[p, :, s].reshape(512, 128).T[0:64].astype(BF16)
            return carry

        lax.fori_loop(0, 2, one, 0)
        write_out.start()

    def spread_all():
        def one(p, carry):
            spread(p, part[p])
            return carry

        lax.fori_loop(0, 2, one, 0)

    for layer in (2, 1):
        e = 5 - layer
        point = top_point if layer == 2 else delta_point(layer)
        edge_faces(e, point)
        send_faces(e)
        if layer == 2:
            whole_act(2)
        whole_delta(point)
        spread_all()
        inner(e)
        conv_inner(e, layer, False)
        correlate(layer)
        sum_0(layer)
        finish(e, layer, False)

    def last_delta(p):
        part[p] = delta_point(0)(p, everywhere)

    all_cells(last_delta)
    spread_all()
    correlate(0)
    sum_0(0)
    sum_1(2)
    sum_1(1)
    store_out()
    sum_2(2)
    sum_2(1)
    sum_1(0)
    sum_2(0)
    for layer in (2, 1, 0):
        sum_3(layer)
    for layer in range(LAYERS):
        sum_end(layer)
        write_sum(layer).wait()
    write_out.wait()


def write_kernel(act, units, out, grads, held, units_in, wide, sems):
    fetch_act = pltpu.make_async_copy(act, held, sems.at[0])
    store_act = pltpu.make_async_copy(held, out, sems.at[1])
    fetch = [
        pltpu.make_async_copy(units.at[layer], units_in.at[layer], sems.at[2 + layer])
        for layer in range(LAYERS)
    ]
    store = [
        pltpu.make_async_copy(wide.at[layer], grads.at[layer], sems.at[2 + LAYERS + layer])
        for layer in range(LAYERS)
    ]
    for copy in fetch:
        copy.start()
    fetch_act.start()
    for layer in range(LAYERS):
        fetch[layer].wait()
        for unit, pair in enumerate(UNIT_KERNELS):
            value = units_in[layer, unit].astype(F32)
            wide[layer, pair[0]] = value[:, 0:64]
            if len(pair) > 1:
                wide[layer, pair[1]] = swap_halves(value)[:, 0:64]
        store[layer].start()
        if layer == 0:
            fetch_act.wait()
            store_act.start()
    for copy in store:
        copy.wait()
    store_act.wait()


def local(features, weights, cotangent, neighbours):
    rows, cols = lax.axis_size("tx"), lax.axis_size("ty")
    vmem = pl.BlockSpec(memory_space=pltpu.VMEM)
    hbm = pl.BlockSpec(memory_space=pltpu.HBM)
    act, units = pl.pallas_call(
        functools.partial(kernel, rows, cols, 1.0 / math.sqrt(4 * rows * cols * BLK**3)),
        out_shape=(
            jax.ShapeDtypeStruct((4, 64, 512), BF16),
            jax.ShapeDtypeStruct((LAYERS, UNITS, 64, 128), BF16),
        ),
        in_specs=[vmem, hbm, hbm, pl.BlockSpec(memory_space=pltpu.SMEM)],
        out_specs=(hbm, hbm),
        scratch_shapes=[
            pltpu.SMEM((4 * 27 * 3,), jnp.int32),
            pltpu.VMEM((5, 64, 8, 128), F32),
            pltpu.VMEM((5, 2, 10, 10, 16, 256), BF16),
            pltpu.VMEM((2, 2, 8, 8, 16, 128), F32),
            pltpu.VMEM((3, 256, 768), BF16),
            pltpu.VMEM((2, 768, 256), BF16),
            pltpu.VMEM((2, 192, 1280), BF16),
            pltpu.VMEM((3, 192, 256), F32),
            pltpu.VMEM((2, 8, 8, 16, 128), F32),
            pltpu.VMEM((4, 5, 8, 128), F32),
            pltpu.VMEM((2, 64, 2, 8, 128), F32),
            pltpu.VMEM((2, 8, 8, 16, 128), F32),
            pltpu.VMEM((LAYERS, 27, 64, 64), BF16),
            pltpu.VMEM((4, 64, 512), BF16),
            pltpu.VMEM((4, 64, 512), BF16),
            pltpu.SemaphoreType.DMA((2,)),
            pltpu.SemaphoreType.DMA((LAYERS + 1,)),
            pltpu.SemaphoreType.DMA((5, 8)),
            pltpu.SemaphoreType.DMA((5, 8)),
            pltpu.SemaphoreType.DMA((LAYERS, 3)),
            pltpu.SemaphoreType.DMA((LAYERS, 3)),
        ]
        + [pltpu.VMEM((2, 9, 32, 128), BF16)] * 10
        + [pltpu.VMEM((4, 16, 128), BF16)] * 5
        + [pltpu.VMEM((4, 16, 128), BF16)] * 5
        + [pltpu.VMEM((UNITS, 64, 128), BF16)] * LAYERS
        + [pltpu.VMEM((cols, 64, 128), BF16)] * LAYERS
        + [pltpu.VMEM((rows, 64, 128), BF16)] * LAYERS
        + [pltpu.VMEM((UNITS, 64, 128), BF16)] * LAYERS,
        compiler_params=pltpu.CompilerParams(
            collective_id=0, has_side_effects=True, vmem_limit_bytes=56 * 1024 * 1024
        ),
    )(features, weights, cotangent, neighbours)
    return pl.pallas_call(
        write_kernel,
        out_shape=(
            jax.ShapeDtypeStruct((4, 64, 512), BF16),
            jax.ShapeDtypeStruct((LAYERS, 27, 64, 64), F32),
        ),
        in_specs=[hbm, hbm],
        out_specs=(hbm, hbm),
        scratch_shapes=[
            pltpu.VMEM((4, 64, 512), BF16),
            pltpu.VMEM((LAYERS, UNITS, 64, 128), BF16),
            pltpu.VMEM((LAYERS, 27, 64, 64), F32),
            pltpu.SemaphoreType.DMA((2 + 2 * LAYERS,)),
        ],
        compiler_params=pltpu.CompilerParams(vmem_limit_bytes=56 * 1024 * 1024),
    )(act, units)


def solution(mesh):
    placed = (P(("tx", "ty"), None, None), P(), P(("tx", "ty"), None, None), P(("tx", "ty"), None))
    return jax.shard_map(
        local,
        mesh=mesh,
        in_specs=placed,
        out_specs=(P(("tx", "ty"), None, None), P()),
        check_vma=False,
    )
```
